256 devices in a mesh: doc: 2 (over core), seq: 32 (over x, z), head: 4 (over y).
Axes of the slice: x: 4, y: 4, z: 8, core: 2. Of those that a mesh axis runs over, the one named last changes fastest.
Arguments:
- att_query: bfloat16 [65536, 2048], P(('doc', 'seq'), 'head'), parts along dimension 0, may hold values from -12 to 12
- att_key: bfloat16 [65536, 2048], P(('doc', 'seq'), 'head'), parts along dimension 0, may hold values from -12 to 12
- att_value: bfloat16 [65536, 2048], P(('doc', 'seq'), 'head'), parts along dimension 0, may hold values from -6 to 6
- delta_query: bfloat16 [65536, 2048], P(('doc', 'seq'), 'head'), parts along dimension 0, may hold values from -6 to 6
- delta_key: bfloat16 [65536, 2048], P(('doc', 'seq'), 'head'), parts along dimension 0, may hold values from -6 to 6
- out_gate: bfloat16 [65536, 2048], P(('doc', 'seq'), 'head'), parts along dimension 0, may hold values from -6 to 6
- log_decay: float32 [16, 65536], P('head', ('doc', 'seq')), parts along dimension 1, may hold values from -1 to 0
- beta: float32 [16, 65536], P('head', ('doc', 'seq')), parts along dimension 1, may hold values from 0 to 1
- norm_gain: float32 [128], replicated, may hold values from 0.1 to 1.9
Outputs:
- layer_output: bfloat16 [65536, 2048], P(('doc', 'seq'), 'head'), parts along dimension 0
The draws below stay inside these ranges and needn't reach their ends.
There are 2 independent parts, one for each index of `doc`. The reference program is written for one: setup_inputs(seed, part) draws one part's arguments, and reference() takes and returns one part's arrays. A program takes and returns all parts, laid end to end along the dimension named above; an argument that names none is the same for every part. Nothing has to cross between parts.
All inputs are finite; a program needn't handle non-finite values.
Results may differ from the reference program's by a relative error of at most 0.0057.
Values may be sent and summed in bfloat16 or wider, within the bound.
No kernel may reach another device: no remote copies, remote signals or barrier semaphores. Data moves between devices by JAX's collectives and lax.ppermute only.
A program may use at most 128 MiB of HBM per device.

```python
import math
import jax
import jax.numpy as jnp
from jax import lax

HEADS = 16
DH = 128
TOK_DEV = 1024
WINDOW = 1024
TOKENS = 32768


def attention_law(key):
    base_key = jax.random.fold_in(key, 3)
    streams = jax.random.split(base_key, 2)
    width = HEADS * DH
    queries = jax.random.normal(streams[0], (TOKENS, width), jnp.float32)
    keyset = jax.random.normal(streams[1], (TOKENS, width), jnp.float32)
    return (jnp.clip(queries, -12.0, 12.0), jnp.clip(keyset, -12.0, 12.0))


def draw_att_query(key, part):
    return attention_law(key)[0].astype(jnp.bfloat16)


def draw_att_key(key, part):
    return attention_law(key)[1].astype(jnp.bfloat16)


def draw_delta_key(key, part):
    key = jax.random.fold_in(key, 11)
    streams = jax.random.split(key, 3)
    shared = jax.random.normal(streams[0], (1, HEADS, DH), jnp.float32)
    jitter = jax.random.normal(streams[1], (TOKENS, HEADS, DH), jnp.float32)
    amount = jax.random.uniform(streams[2], (TOKENS, HEADS, 1), jnp.float32, 0.8, 1.4)
    combined = jnp.clip(amount * shared + jitter, -6.0, 6.0)
    return combined.reshape(TOKENS, HEADS * DH).astype(jnp.bfloat16)


def gate_law(key):
    base_key = jax.random.fold_in(key, 7)
    streams = jax.random.split(base_key, 12)
    order = jax.random.permutation(streams[0], HEADS)
    slow_count = HEADS // 2
    fast_count = HEADS // 4
    slow_heads = (order < slow_count)[:, None]
    fast_heads = (order >= HEADS - fast_count)[:, None]
    decay_spread = jnp.exp(jax.random.uniform(streams[1], (HEADS, 1), jnp.float32, math.log(0.05), math.log(0.2)))
    block_count = TOKENS // TOK_DEV
    device_factor = jnp.repeat(jnp.exp(jax.random.uniform(streams[2], (HEADS, block_count), jnp.float32, -0.35, 0.35)), TOK_DEV, axis=1)
    roughness = jnp.exp(jax.random.uniform(streams[3], (HEADS, TOKENS), jnp.float32, math.log(0.6), math.log(1.4)))
    fast_rate = 1.0 / jax.random.uniform(streams[4], (HEADS, 1), jnp.float32, 30.0, 50.0)
    medium_rate = 1.0 / jax.random.uniform(streams[10], (HEADS, 1), jnp.float32, 200.0, 400.0)
    base_rate = jnp.where(slow_heads, decay_spread / TOKENS, jnp.where(fast_heads, fast_rate, medium_rate))
    forgetting_factors = base_rate * device_factor * roughness
    element_indices = jax.random.randint(streams[5], (HEADS, 2), 0, TOKENS)
    sequence_positions = jnp.arange(TOKENS, dtype=jnp.int32)
    segment_spans = jnp.any(sequence_positions[None, None, :] == element_indices[:, :, None], axis=1)
    forgetting_steps = jax.random.uniform(streams[6], (HEADS, TOKENS), jnp.float32, 0.22, 0.69)
    logarithmic_forgetting = -(forgetting_factors + jnp.where(segment_spans, forgetting_steps, 0.0))
    write_spread = jnp.exp(jax.random.uniform(streams[7], (HEADS, 1), jnp.float32, math.log(2.5), math.log(4.5)))
    write_rough = jax.random.uniform(streams[8], (HEADS, TOKENS), jnp.float32, 0.6, 1.4)
    slow_beta = jnp.minimum(write_spread * DH / TOKENS * write_rough, 0.95)
    fast_beta = jax.random.uniform(streams[9], (HEADS, TOKENS), jnp.float32, 0.25, 0.95)
    medium_beta = jax.random.uniform(streams[11], (HEADS, TOKENS), jnp.float32, 0.05, 0.3)
    betas = jnp.where(slow_heads, slow_beta, jnp.where(fast_heads, fast_beta, medium_beta))
    return (logarithmic_forgetting, betas)


def draw_log_decay(key, part):
    return gate_law(key)[0]


def draw_beta(key, part):
    return gate_law(key)[1]


def steps_of(key, shape, cuts, least, largest):
    def one(dim, blocks):
        steps = jax.random.uniform(jax.random.fold_in(jax.random.fold_in(key, 6), dim), (blocks,), jnp.float32, least / len(cuts), largest / len(cuts))
        return jnp.repeat(jnp.exp(steps), shape[dim] // blocks).reshape((-1,) + (1,) * (len(shape) - dim - 1))

    loudness = one(*cuts[0])
    for cut in cuts[1:]:
        loudness = loudness * one(*cut)
    return loudness


def gaussian(key, shape, spread, limit, shards=(), held_as=jnp.bfloat16):
    factor_of = steps_of(key, shape, shards, -0.22, 0.18) if shards else 1.0
    drawn = jax.random.normal(key, shape, jnp.float32) * spread * factor_of
    return jnp.minimum(jnp.maximum(drawn, -limit), limit).astype(held_as)


def setup_inputs(seed: int = 0, part: int = 0) -> dict:
    arg_keys = jax.random.split(jax.random.key(seed), 10)
    own_keys = jax.random.split(jax.random.fold_in(arg_keys[9], part), 10)
    return {
        "att_query": draw_att_query(jax.random.fold_in(jax.random.fold_in(arg_keys[9], part), 71), part),
        "att_key": draw_att_key(jax.random.fold_in(jax.random.fold_in(arg_keys[9], part), 71), part),
        "att_value": gaussian(own_keys[2], (TOKENS, HEADS * DH), 1.0, 6.0, ((0, 32), (1, 4))),
        "delta_query": gaussian(own_keys[3], (TOKENS, HEADS * DH), 1.0, 6.0, ((0, 32), (1, 4))),
        "delta_key": draw_delta_key(jax.random.fold_in(jax.random.fold_in(arg_keys[9], part), 71), part),
        "out_gate": gaussian(own_keys[5], (TOKENS, HEADS * DH), 1.0, 6.0, ((0, 32), (1, 4))),
        "log_decay": draw_log_decay(jax.random.fold_in(jax.random.fold_in(arg_keys[9], part), 71), part),
        "beta": draw_beta(jax.random.fold_in(jax.random.fold_in(arg_keys[9], part), 71), part),
        "norm_gain": jnp.clip(1.0 + 0.18 * jax.random.normal(arg_keys[8], (DH,), jnp.float32), 0.1, 1.9),
    }


PRECISE = lax.Precision.HIGHEST

def unit_rows(tensor):
    return tensor / jnp.sqrt(lax.optimization_barrier(jnp.sum(tensor * tensor, axis=-1, keepdims=True)) + 1e-06)

def rms_rows(tensor):
    return tensor / jnp.sqrt(lax.optimization_barrier(jnp.mean(tensor * tensor, axis=-1, keepdims=True)) + 1e-06)

def attend_all(query_rows, key_rows, value_rows):
    block_rows = min(512, TOK_DEV)
    block_count = TOKENS // block_rows
    scale = 1.0 / math.sqrt(DH)
    padding = jnp.zeros((WINDOW, HEADS, DH), jnp.float32)
    key_padded = jnp.concatenate([padding, key_rows.astype(jnp.float32)], axis=0)
    value_padded = jnp.concatenate([padding, value_rows.astype(jnp.float32)], axis=0)
    query_float = query_rows.astype(jnp.float32)

    def one_block(block_index):
        first_row = block_index * block_rows
        query_block = lax.dynamic_slice_in_dim(query_float, first_row, block_rows, 0)
        key_block = lax.dynamic_slice_in_dim(key_padded, first_row, block_rows + WINDOW, 0)
        value_block = lax.dynamic_slice_in_dim(value_padded, first_row, block_rows + WINDOW, 0)
        offsets = jnp.arange(block_rows, dtype=jnp.int32)[:, None] + WINDOW - jnp.arange(block_rows + WINDOW, dtype=jnp.int32)[None, :]
        key_place = first_row - WINDOW + jnp.arange(block_rows + WINDOW, dtype=jnp.int32)
        allowed = (offsets >= 0) & (offsets < WINDOW) & (key_place[None, :] >= 0)
        scores = jnp.einsum('qhd,khd->hqk', query_block, key_block) * scale
        masked = jnp.where(allowed[None], scores, -1e+30)
        summit = lax.optimization_barrier(jnp.max(masked, axis=-1, keepdims=True))
        powered = jnp.where(allowed[None], jnp.exp(masked - summit), 0.0)
        denominator = lax.optimization_barrier(jnp.sum(powered, axis=-1))
        weights = lax.optimization_barrier(powered.astype(jnp.bfloat16)).astype(jnp.float32)
        blended = jnp.einsum('hqk,khd->qhd', weights, value_block) / jnp.transpose(denominator)[:, :, None]
        return blended.astype(jnp.bfloat16)
    blocks = lax.map(one_block, jnp.arange(block_count, dtype=jnp.int32))
    return blocks.reshape(TOKENS, HEADS, DH)

def reference(att_query, att_key, att_value, delta_query, delta_key, out_gate, log_decay, beta, norm_gain):
    shape_three = (TOKENS, HEADS, DH)
    attended = attend_all(att_query.reshape(shape_three), att_key.reshape(shape_three), att_value.reshape(shape_three))
    values = rms_rows(attended.astype(jnp.float32))
    unit_keys = unit_rows(delta_key.reshape(shape_three).astype(jnp.float32))
    unit_queries = unit_rows(delta_query.reshape(shape_three).astype(jnp.float32))

    def advance(carried, inputs):
        query_row, key_row, value_row, log_row, beta_row = inputs
        kept = jnp.exp(log_row)[:, None, None] * carried
        predicted = jnp.einsum('hvd,hd->hv', kept, key_row, precision=PRECISE)
        carried = kept + jnp.einsum('hv,hd->hvd', beta_row[:, None] * (value_row - predicted), key_row, precision=PRECISE)
        readout = jnp.einsum('hvd,hd->hv', carried, query_row, precision=PRECISE)
        return (carried, readout)
    starting = jnp.zeros((HEADS, DH, DH), jnp.float32)
    inputs = (unit_queries, unit_keys, values, jnp.transpose(log_decay), jnp.transpose(beta))
    final_state, readouts = lax.scan(advance, starting, inputs)
    gates = jax.nn.silu(out_gate.reshape(shape_three).astype(jnp.float32))
    rescaled_output = rms_rows(readouts) * norm_gain * gates
    return rescaled_output.reshape(TOKENS, HEADS * DH).astype(jnp.bfloat16)
```

```python
import functools
import math

import jax
import jax.numpy as jnp
from jax import lax
from jax.experimental import pallas as pl
from jax.experimental.pallas import tpu as pltpu
from jax.sharding import PartitionSpec as P

CHUNK = 128
DH = 128
WIRE = 144
VMEM = 60 * 2**20
NEG = -1e30
F32 = jnp.float32
BF16 = jnp.bfloat16
NN = (((1,), (0,)), ((), ()))
NT = (((1,), (1,)), ((), ()))


def dot(a, b, dims=NN):
    return lax.dot_general(a, b, dims, preferred_element_type=F32)


def shift_lanes(row, steps):
    lane = lax.broadcasted_iota(jnp.int32, row.shape, 1)
    return jnp.where(lane >= steps, pltpu.roll(row, steps, axis=1), 0.0)


def halves(value):
    high = value.astype(BF16)
    return high, (value - high.astype(F32)).astype(BF16)


def beside(*parts):
    return jnp.concatenate(parts, axis=1)


def below(*parts):
    return jnp.concatenate(parts, axis=0)


def split_three(g):
    high = g.astype(BF16)
    rest = g - high.astype(F32)
    mid = rest.astype(BF16)
    low = (rest - mid.astype(F32)).astype(BF16)
    return high, mid, low


def pack_gain(g):
    row = lax.broadcasted_iota(jnp.int32, (WIRE - DH, DH), 0)
    high, mid, low = split_three(g)
    block = jnp.where(
        row == 0,
        high.astype(F32),
        jnp.where(row == 1, mid.astype(F32), jnp.where(row == 2, low.astype(F32), 0.0)),
    )
    return block.astype(BF16)


def unpack_gain(block):
    rows = block.astype(F32)
    return rows[0:1] + rows[1:2] + rows[2:3]


def prep_kernel(
    heads, ld_ref, be_ref, k_ref, q_ref, m_ref, ke_ref, qe_ref, qf_ref, e_ref, g_ref, w_ref, f_scr, gp_scr
):
    c = pl.program_id(0)

    @pl.when(c == 0)
    def _():
        f_scr[...] = jnp.zeros_like(f_scr)
        gp_scr[...] = jnp.ones_like(gp_scr)

    rows = jnp.concatenate([ld_ref[...], be_ref[...]], axis=0)
    cum = rows
    for steps in (1, 2, 4, 8, 16, 32, 64):
        cum = cum + shift_lanes(cum, steps)
    row8 = lax.broadcasted_iota(jnp.int32, (2 * heads, CHUNK), 0)
    rows = jnp.where(row8 < heads, cum, rows)
    cols = jnp.transpose(rows)
    ti = lax.broadcasted_iota(jnp.int32, (CHUNK, CHUNK), 0)
    tj = lax.broadcasted_iota(jnp.int32, (CHUNK, CHUNK), 1)
    eye = jnp.where(ti == tj, 1.0, 0.0)
    keys = []
    inv_k = []
    colmat = jnp.zeros((CHUNK, CHUNK), F32)
    for h in range(heads):
        k = k_ref[:, h * DH : (h + 1) * DH]
        kf = k.astype(F32)
        rk = 1.0 / jnp.sqrt(jnp.sum(kf * kf, axis=1, keepdims=True) + 1e-6)
        keys.append((k, kf))
        inv_k.append(rk)
        colmat = jnp.where(tj == h, rk, colmat)
    rowmat = jnp.transpose(colmat)
    state = []
    for h in range(heads):
        k, kf = keys[h]
        rk_c = inv_k[h]
        rk_r = rowmat[h : h + 1]
        q = q_ref[:, h * DH : (h + 1) * DH]
        qf = q.astype(F32)
        rq_c = 1.0 / jnp.sqrt(jnp.sum(qf * qf, axis=1, keepdims=True) + 1e-6)
        g_c = cols[:, h : h + 1]
        g_r = rows[h : h + 1]
        b_c = cols[:, heads + h : heads + h + 1]
        b_r = rows[heads + h : heads + h + 1]
        decay = jnp.exp(jnp.where(ti >= tj, g_c - g_r, NEG)) * rk_r
        kk = dot(k, k, NT)
        qk = dot(q, k, NT)
        a = beside(*halves(decay * rq_c * qk))
        low = jnp.where(ti > tj, decay * (b_c * rk_c) * kk, 0.0)
        t = eye - jnp.where((ti >> 1) == (tj >> 1), low, 0.0)
        state.append((k, kf, rk_c, rk_r, qf, rq_c, g_c, g_r, b_r, a, low, t))
    ts = [s[-1] for s in state]
    for shift in range(1, 7):
        pair = (ti >> (shift + 1)) == (tj >> (shift + 1))
        cross = pair & (((ti >> shift) & 1) == 1) & (((tj >> shift) & 1) == 0)
        tb = [t.astype(BF16) for t in ts]
        lm = [below(*halves(jnp.where(cross, s[-2], 0.0))) for s in state]
        mid = [dot(beside(x, x), y).astype(BF16) for x, y in zip(tb, lm)]
        ts = [t - dot(x, y) for t, x, y in zip(ts, mid, tb)]
    for h in range(heads):
        k, kf, rk_c, rk_r, qf, rq_c, g_c, g_r, b_r, a, low, _ = state[h]
        t = ts[h]
        g_end = g_r[:, CHUNK - 1 : CHUNK]
        tail_c = jnp.exp(g_end - g_c)
        w = dot((t * (b_r * jnp.exp(g_r) * rk_r)).astype(BF16), k)
        wb = w.astype(BF16)
        tw = beside(t.astype(BF16), wb)
        both = dot(a, below(tw, tw))
        m_ref[0, h] = (both[:, :CHUNK] * b_r).astype(BF16)
        qe = (jnp.exp(g_c) * rq_c) * qf - both[:, CHUNK:]
        qeb = qe.astype(BF16)
        kt = jnp.transpose(kf).astype(BF16)
        ke = dot(beside(kt, kt), below(*halves((tail_c * rk_c) * t * b_r)))
        ke_ref[0, h] = beside(*halves(ke))
        e = -dot(kt, ((tail_c * rk_c) * w).astype(BF16))
        eb = e.astype(BF16)
        gc = jnp.broadcast_to(jnp.exp(g_end), (1, DH))
        gp = gp_scr[h : h + 1]
        f = f_scr[h]
        fb = f.astype(BF16)
        qe_ref[0, h] = qeb
        qf_ref[0, h] = (gp * qe + dot(qeb, fb)).astype(BF16)
        e_ref[0, h] = eb
        f_new = gc * f + gp * e + dot(eb, fb)
        gp_new = gp * gc
        f_scr[h] = f_new
        gp_scr[h : h + 1] = gp_new
        g_ref[0, h : h + 1] = gc

        @pl.when(c == pl.num_programs(0) - 1)
        def _():
            w_ref[h, :DH] = jnp.transpose(f_new).astype(BF16)
            w_ref[h, DH:] = pack_gain(gp_new)


def prep(log_decay, beta, delta_key, delta_query):
    heads, rows = log_decay.shape
    chunks = rows // CHUNK
    big = jax.ShapeDtypeStruct((chunks, heads, CHUNK, DH), BF16)
    big_spec = pl.BlockSpec((1, heads, CHUNK, DH), lambda c: (c, 0, 0, 0))
    row_spec = pl.BlockSpec((heads, CHUNK), lambda c: (0, c))
    tok_spec = pl.BlockSpec((CHUNK, heads * DH), lambda c: (c, 0))
    return pl.pallas_call(
        functools.partial(prep_kernel, heads),
        grid=(chunks,),
        in_specs=[row_spec, row_spec, tok_spec, tok_spec],
        out_specs=[big_spec, pl.BlockSpec((1, heads, CHUNK, 2 * DH), lambda c: (c, 0, 0, 0))]
        + [big_spec] * 3
        + [
            pl.BlockSpec((1, heads, DH), lambda c: (c, 0, 0)),
            pl.BlockSpec((heads, WIRE, DH), lambda c: (0, 0, 0)),
        ],
        out_shape=[big, jax.ShapeDtypeStruct((chunks, heads, CHUNK, 2 * DH), BF16)]
        + [big] * 3
        + [
            jax.ShapeDtypeStruct((chunks, heads, DH), F32),
            jax.ShapeDtypeStruct((heads, WIRE, DH), BF16),
        ],
        scratch_shapes=[pltpu.VMEM((heads, DH, DH), F32), pltpu.VMEM((heads, DH), F32)],
        compiler_params=pltpu.CompilerParams(vmem_limit_bytes=VMEM),
        cost_estimate=pl.CostEstimate(flops=1_000_000, bytes_accessed=1_000_000, transcendentals=0),
        name="delta_prep",
    )(log_decay, beta, delta_key, delta_query)


QB = 256


def attend_kernel(
    window,
    first_ref,
    q_ref,
    kp_ref,
    ko_ref,
    vp_ref,
    vo_ref,
    m_ref,
    ke_ref,
    qe_ref,
    e_ref,
    g_ref,
    r_ref,
    b_ref,
    kx,
    vx,
    x_scr,
):
    h = pl.program_id(0)
    i = pl.program_id(1)
    first = first_ref[0]

    @pl.when(i == 0)
    def _():
        kx[window:] = ko_ref[...]
        vx[window:, :DH] = vo_ref[...]
        vx[window:, DH:] = jnp.ones((vo_ref.shape[0], DH), BF16)
        vx[:window, :DH] = vp_ref[...]
        x_scr[...] = jnp.zeros_like(x_scr)

        @pl.when(first == 0)
        def _():
            kx[:window] = kp_ref[...]
            vx[:window, DH:] = jnp.ones((window, DH), BF16)

        @pl.when(first != 0)
        def _():
            kx[:window] = jnp.broadcast_to(ko_ref[0:1].astype(F32), (window, DH)).astype(BF16)
            vx[:window, DH:] = jnp.zeros((window, DH), BF16)

    start = pl.multiple_of(i * QB, QB)
    span = window + QB
    keys = kx[pl.ds(start, span)]
    vals = vx[pl.ds(start, span)]
    scale = 1.0 / math.sqrt(DH) * math.log2(math.e)
    s = dot(q_ref[...], keys, NT)
    ri = lax.broadcasted_iota(jnp.int32, (QB, QB), 0)
    rj = lax.broadcasted_iota(jnp.int32, (QB, QB), 1)
    s = jnp.concatenate(
        [
            jnp.where(rj > ri, s[:, :QB], NEG),
            s[:, QB:window],
            jnp.where(rj <= ri, s[:, window:], NEG),
        ],
        axis=1,
    )
    top = jnp.max(s, axis=1, keepdims=True)
    p = jnp.exp2((s - top) * scale).astype(BF16)
    pv = dot(p, vals)
    o = (pv[:, :DH] / pv[:, DH:]).astype(BF16).astype(F32)
    vh, vl = halves(o / jnp.sqrt(jnp.mean(o * o, axis=1, keepdims=True) + 1e-6))
    x = x_scr[...]
    for cc in range(QB // CHUNK):
        part = slice(cc * CHUNK, (cc + 1) * CHUNK)
        xh, xl = halves(x)
        m, qe, ke = m_ref[cc, 0], qe_ref[cc, 0], ke_ref[cc, 0]
        r_ref[part] = dot(beside(m, m), below(vh[part], vl[part])) + dot(beside(qe, qe), below(xh, xl))
        fresh = dot(ke, below(vh[part], vh[part])) + dot(ke[:, :DH], vl[part])
        x = g_ref[cc, pl.ds(h, 1)] * x + dot(e_ref[cc, 0], xh) + fresh
    x_scr[...] = x

    @pl.when(i == pl.num_programs(1) - 1)
    def _():
        b_ref[0] = jnp.transpose(x).astype(BF16)


def attend(first, att_query, k_prev, k_own, v_prev, v_own, m, ke, qe, e, g):
    rows, width = att_query.shape
    heads = width // DH
    window = k_prev.shape[0]
    per = QB // CHUNK
    col = lambda h, i: (0, h)
    big = pl.BlockSpec((per, 1, CHUNK, DH), lambda h, i: (i, h, 0, 0))
    return pl.pallas_call(
        functools.partial(attend_kernel, window),
        grid=(heads, rows // QB),
        in_specs=[
            pl.BlockSpec(memory_space=pltpu.SMEM),
            pl.BlockSpec((QB, DH), lambda h, i: (i, h)),
            pl.BlockSpec((window, DH), col),
            pl.BlockSpec((rows, DH), col),
            pl.BlockSpec((window, DH), col),
            pl.BlockSpec((rows, DH), col),
            big,
            pl.BlockSpec((per, 1, CHUNK, 2 * DH), lambda h, i: (i, h, 0, 0)),
            big,
            big,
            pl.BlockSpec((per, heads, DH), lambda h, i: (i, 0, 0)),
        ],
        out_specs=[
            pl.BlockSpec((QB, DH), lambda h, i: (i, h)),
            pl.BlockSpec((1, DH, DH), lambda h, i: (h, 0, 0)),
        ],
        out_shape=[
            jax.ShapeDtypeStruct((rows, width), F32),
            jax.ShapeDtypeStruct((heads, DH, DH), BF16),
        ],
        scratch_shapes=[
            pltpu.VMEM((window + rows, DH), BF16),
            pltpu.VMEM((window + rows, 2 * DH), BF16),
            pltpu.VMEM((DH, DH), F32),
        ],
        compiler_params=pltpu.CompilerParams(vmem_limit_bytes=VMEM),
        cost_estimate=pl.CostEstimate(
            flops=1_000_000_000_000, bytes_accessed=14_000_000, transcendentals=5_000_000
        ),
        name="window_attention",
    )(first, att_query, k_prev, k_own, v_prev, v_own, m, ke, qe, e, g)


def prefix_kernel(minor, majors, d_ref, p_ref):
    ti = lax.broadcasted_iota(jnp.int32, (DH, DH), 0)
    gs = [jnp.ones((1, DH), F32) for _ in range(majors)]
    fs = [jnp.zeros((DH, DH), F32) for _ in range(majors)]
    for z in range(minor + 1):
        for k in range(majors):
            p_ref[k, z, :DH] = fs[k].astype(BF16)
            p_ref[k, z, DH:] = pack_gain(gs[k])
        if z == minor:
            break
        for k in range(majors):
            d = d_ref[z, k, :DH]
            g = unpack_gain(d_ref[z, k, DH:])
            fs[k] = g * fs[k] + gs[k] * d.astype(F32) + dot(fs[k].astype(BF16), d)
            gs[k] = gs[k] * g


def prefix(d_all):
    minor, majors = d_all.shape[:2]
    return pl.pallas_call(
        functools.partial(prefix_kernel, minor, majors),
        in_specs=[pl.BlockSpec(memory_space=pltpu.VMEM)],
        out_specs=pl.BlockSpec(memory_space=pltpu.VMEM),
        out_shape=jax.ShapeDtypeStruct((majors, minor + 1, WIRE, DH), BF16),
        compiler_params=pltpu.CompilerParams(vmem_limit_bytes=VMEM),
        cost_estimate=pl.CostEstimate(flops=140_000_000, bytes_accessed=3_000_000, transcendentals=0),
        name="decay_prefix",
    )(d_all)


def chain_kernel(minor, majors, d_ref, p_ref, b_ref, s_ref):
    size = b_ref.shape[1]
    local = [[] for _ in range(majors)]
    acc = [jnp.zeros((size, DH), F32) for _ in range(majors)]
    for z in range(minor):
        for x in range(majors):
            local[x].append(acc[x])
            g = unpack_gain(d_ref[z, x, DH:])
            b = b_ref[x * minor + z].astype(F32)
            acc[x] = g * acc[x] + b + dot(acc[x].astype(BF16), d_ref[z, x, :DH])
    start = jnp.zeros((size, DH), F32)
    for x in range(majors):
        high = start.astype(BF16)
        for z in range(minor):
            g = unpack_gain(p_ref[x, z, DH:])
            out = g * start + local[x][z] + dot(high, p_ref[x, z, :DH])
            s_ref[x * minor + z] = out.astype(BF16)
        g = unpack_gain(p_ref[x, minor, DH:])
        start = g * start + acc[x] + dot(high, p_ref[x, minor, :DH])


def chain(d_all, p_all, b_rows):
    minor, majors = d_all.shape[:2]
    vm = pl.BlockSpec(memory_space=pltpu.VMEM)
    return pl.pallas_call(
        functools.partial(chain_kernel, minor, majors),
        in_specs=[vm, vm, vm],
        out_specs=vm,
        out_shape=jax.ShapeDtypeStruct(b_rows.shape, BF16),
        compiler_params=pltpu.CompilerParams(vmem_limit_bytes=VMEM),
        cost_estimate=pl.CostEstimate(flops=40_000_000, bytes_accessed=4_000_000, transcendentals=0),
        name="state_chain",
    )(d_all, p_all, b_rows)


def finish_kernel(heads, r_ref, qf_ref, s_ref, gate_ref, gain_ref, o_ref):
    gain = gain_ref[...]
    for h in range(heads):
        cols = slice(h * DH, (h + 1) * DH)
        r = r_ref[:, cols] + dot(qf_ref[0, h], s_ref[h], NT)
        gate = gate_ref[:, cols].astype(F32)
        r = r / jnp.sqrt(jnp.mean(r * r, axis=1, keepdims=True) + 1e-6)
        o_ref[:, cols] = (r * gain * (gate / (1.0 + jnp.exp(-gate)))).astype(BF16)


def finish(readout, qf, state, out_gate, gain):
    rows, width = readout.shape
    heads = width // DH
    tok = pl.BlockSpec((CHUNK, width), lambda c: (c, 0))
    return pl.pallas_call(
        functools.partial(finish_kernel, heads),
        grid=(rows // CHUNK,),
        in_specs=[
            tok,
            pl.BlockSpec((1, heads, CHUNK, DH), lambda c: (c, 0, 0, 0)),
            pl.BlockSpec((heads, DH, DH), lambda c: (0, 0, 0)),
            tok,
            pl.BlockSpec((1, DH), lambda c: (0, 0)),
        ],
        out_specs=tok,
        out_shape=jax.ShapeDtypeStruct((rows, width), BF16),
        compiler_params=pltpu.CompilerParams(vmem_limit_bytes=VMEM),
        cost_estimate=pl.CostEstimate(flops=140_000_000, bytes_accessed=6_000_000, transcendentals=600_000),
        name="gated_readout",
    )(readout, qf, state, out_gate, gain)


def body(att_query, att_key, att_value, delta_query, delta_key, out_gate, log_decay, beta, norm_gain):
    heads = log_decay.shape[0]
    count = lax.axis_size("seq")
    majors = heads
    minor = count // majors
    place = lax.axis_index("seq")
    onward = [(s, s + 1) for s in range(count - 1)]
    k_prev = lax.ppermute(att_key, "seq", onward)
    v_prev = lax.ppermute(att_value, "seq", onward)
    m, ke, qe, qf, e, g, wire = prep(log_decay, beta, delta_key, delta_query)
    columns = [[x * minor + z for x in range(majors)] for z in range(minor)]
    lines = [[x * minor + z for z in range(minor)] for x in range(majors)]
    pieces = lax.all_to_all(wire, "seq", 0, 0, axis_index_groups=columns)
    d_all = lax.all_gather(pieces, "seq", axis_index_groups=lines)
    p_all = prefix(d_all)
    first = jnp.reshape((place == 0).astype(jnp.int32), (1,))
    readout, b = attend(first, att_query, k_prev, att_key, v_prev, att_value, m, ke, qe, e, g)
    b, p_all = lax.optimization_barrier((b, p_all))
    b_rows = lax.all_to_all(b.reshape(count, heads * DH // count, DH), "seq", 0, 0)
    s_rows = chain(d_all, p_all, b_rows)
    state = lax.all_to_all(s_rows, "seq", 0, 0).reshape(heads, DH, DH)
    return finish(readout, qf, state, out_gate, norm_gain.reshape(1, DH))


def solution(mesh):
    tokens = P(("doc", "seq"), "head")
    gates = P("head", ("doc", "seq"))
    return jax.shard_map(
        body,
        mesh=mesh,
        in_specs=(tokens,) * 6 + (gates, gates, P()),
        out_specs=tokens,
        check_vma=False,
    )
```

```python
import functools
import math

import jax
import jax.numpy as jnp
from jax import lax
from jax.experimental import pallas as pl
from jax.experimental.pallas import tpu as pltpu
from jax.sharding import PartitionSpec as P

CHUNK = 128
DH = 128
WIRE = 144
VMEM = 60 * 2**20
MIDDLE = 58 * 2**20
SMALL = 8 * 2**20
NEG = -1e30
F32 = jnp.float32
BF16 = jnp.bfloat16
NN = (((1,), (0,)), ((), ()))
NT = (((1,), (1,)), ((), ()))


def dot(a, b, dims=NN):
    return lax.dot_general(a, b, dims, preferred_element_type=F32)


def shift_lanes(row, steps):
    lane = lax.broadcasted_iota(jnp.int32, row.shape, 1)
    return jnp.where(lane >= steps, pltpu.roll(row, steps, axis=1), 0.0)


def halves(value):
    high = value.astype(BF16)
    return high, (value - high.astype(F32)).astype(BF16)


def beside(*parts):
    return jnp.concatenate(parts, axis=1)


def below(*parts):
    return jnp.concatenate(parts, axis=0)


def split_three(g):
    high = g.astype(BF16)
    rest = g - high.astype(F32)
    mid = rest.astype(BF16)
    low = (rest - mid.astype(F32)).astype(BF16)
    return high, mid, low


def pack_gain(g):
    row = lax.broadcasted_iota(jnp.int32, (WIRE - DH, DH), 0)
    high, mid, low = split_three(g)
    block = jnp.where(
        row == 0,
        high.astype(F32),
        jnp.where(row == 1, mid.astype(F32), jnp.where(row == 2, low.astype(F32), 0.0)),
    )
    return block.astype(BF16)


def unpack_gain(block):
    rows = block.astype(F32)
    return rows[0:1] + rows[1:2] + rows[2:3]


def gate_rows(heads, ld, be):
    rows = below(ld, be)
    cum = rows
    for steps in (1, 2, 4, 8, 16, 32, 64):
        cum = cum + shift_lanes(cum, steps)
    row8 = lax.broadcasted_iota(jnp.int32, (2 * heads, CHUNK), 0)
    return jnp.where(row8 < heads, cum, rows)


def prep_kernel(
    heads, per, ld_ref, be_ref, k_ref, q_ref, m_ref, ke_ref, qe_ref, qf_ref, e_ref, g_ref, w_ref, f_scr, gp_scr
):
    step = pl.program_id(0)

    @pl.when(step == 0)
    def _():
        f_scr[...] = jnp.zeros_like(f_scr)
        gp_scr[...] = jnp.ones_like(gp_scr)

    ti = lax.broadcasted_iota(jnp.int32, (CHUNK, CHUNK), 0)
    tj = lax.broadcasted_iota(jnp.int32, (CHUNK, CHUNK), 1)
    eye = jnp.where(ti == tj, 1.0, 0.0)
    state = []
    ts = []
    for c in range(per):
        part = slice(c * CHUNK, (c + 1) * CHUNK)
        rows = gate_rows(heads, ld_ref[:, part], be_ref[:, part])
        cols = jnp.transpose(rows)
        keys = []
        colmat = jnp.zeros((CHUNK, CHUNK), F32)
        for h in range(heads):
            k = k_ref[part, h * DH : (h + 1) * DH]
            kf = k.astype(F32)
            rk = lax.rsqrt(jnp.sum(kf * kf, axis=1, keepdims=True) + 1e-6)
            keys.append((k, kf, rk))
            colmat = jnp.where(tj == h, rk, colmat)
        rowmat = jnp.transpose(colmat)
        for h in range(heads):
            k, kf, rk_c = keys[h]
            rk_r = rowmat[h : h + 1]
            q = q_ref[part, h * DH : (h + 1) * DH]
            qf = q.astype(F32)
            rq_c = lax.rsqrt(jnp.sum(qf * qf, axis=1, keepdims=True) + 1e-6)
            g_c = cols[:, h : h + 1]
            g_r = rows[h : h + 1]
            b_c = cols[:, heads + h : heads + h + 1]
            b_r = rows[heads + h : heads + h + 1]
            decay = jnp.exp(jnp.where(ti >= tj, g_c - g_r, NEG)) * rk_r
            kk = dot(k, k, NT)
            qk = dot(q, k, NT)
            a = beside(*halves(decay * rq_c * qk))
            low = jnp.where(ti > tj, decay * (b_c * rk_c) * kk, 0.0)
            ts.append(eye - jnp.where((ti >> 1) == (tj >> 1), low, 0.0))
            state.append((k, kf, rk_c, rk_r, qf, rq_c, g_c, g_r, b_r, a, low))
    for shift in range(1, 7):
        pair = (ti >> (shift + 1)) == (tj >> (shift + 1))
        cross = pair & (((ti >> shift) & 1) == 1) & (((tj >> shift) & 1) == 0)
        tb = [t.astype(BF16) for t in ts]
        lm = [below(*halves(jnp.where(cross, s[-1], 0.0))) for s in state]
        mid = [dot(beside(x, x), y).astype(BF16) for x, y in zip(tb, lm)]
        ts = [t - dot(x, y) for t, x, y in zip(ts, mid, tb)]
    for c in range(per):
        for h in range(heads):
            k, kf, rk_c, rk_r, qf, rq_c, g_c, g_r, b_r, a, low = state[c * heads + h]
            t = ts[c * heads + h]
            g_end = g_r[:, CHUNK - 1 : CHUNK]
            tail_c = jnp.exp(g_end - g_c) * rk_c
            w = dot((t * (b_r * jnp.exp(g_r) * rk_r)).astype(BF16), k)
            wb = w.astype(BF16)
            tw = beside(t.astype(BF16), wb)
            both = dot(a, below(tw, tw))
            m_ref[c, h] = (both[:, :CHUNK] * b_r).astype(BF16)
            qe = (jnp.exp(g_c) * rq_c) * qf - both[:, CHUNK:]
            qeb = qe.astype(BF16)
            kt = jnp.transpose(kf).astype(BF16)
            ke = dot(beside(kt, kt), below(*halves(tail_c * t * b_r)))
            ke_ref[c, h] = beside(*halves(ke))
            e = -dot(kt, (tail_c * w).astype(BF16))
            eb = e.astype(BF16)
            gc = jnp.broadcast_to(jnp.exp(g_end), (1, DH))
            gp = gp_scr[h : h + 1]
            f = f_scr[h]
            fb = f.astype(BF16)
            qe_ref[c, h] = qeb
            qf_ref[c, h] = beside(*halves(gp * qe + dot(qeb, fb)))
            e_ref[c, h] = eb
            f_scr[h] = gc * f + gp * e + dot(eb, fb)
            gp_scr[h : h + 1] = gp * gc
            g_ref[c, h : h + 1] = gc

    @pl.when(step == pl.num_programs(0) - 1)
    def _():
        for h in range(heads):
            matrix = jnp.transpose(f_scr[h]).astype(BF16)
            gain = pack_gain(gp_scr[h : h + 1])
            for copy in range(w_ref.shape[0] // heads):
                w_ref[h * (w_ref.shape[0] // heads) + copy, :DH] = matrix
                w_ref[h * (w_ref.shape[0] // heads) + copy, DH:] = gain


PER = 4


def prep(log_decay, beta, delta_key, delta_query, copies):
    heads, rows = log_decay.shape
    chunks = rows // CHUNK
    big = jax.ShapeDtypeStruct((chunks, heads, CHUNK, DH), BF16)
    wide = jax.ShapeDtypeStruct((chunks, heads, CHUNK, 2 * DH), BF16)
    big_spec = pl.BlockSpec((PER, heads, CHUNK, DH), lambda c: (c, 0, 0, 0))
    wide_spec = pl.BlockSpec((PER, heads, CHUNK, 2 * DH), lambda c: (c, 0, 0, 0))
    row_spec = pl.BlockSpec((heads, PER * CHUNK), lambda c: (0, c))
    tok_spec = pl.BlockSpec((PER * CHUNK, heads * DH), lambda c: (c, 0))
    return pl.pallas_call(
        functools.partial(prep_kernel, heads, PER),
        grid=(chunks // PER,),
        in_specs=[row_spec, row_spec, tok_spec, tok_spec],
        out_specs=[big_spec, wide_spec, big_spec, wide_spec, big_spec]
        + [
            pl.BlockSpec((PER, heads, DH), lambda c: (c, 0, 0)),
            pl.BlockSpec((heads * copies, WIRE, DH), lambda c: (0, 0, 0)),
        ],
        out_shape=[big, wide, big, wide, big]
        + [
            jax.ShapeDtypeStruct((chunks, heads, DH), F32),
            jax.ShapeDtypeStruct((heads * copies, WIRE, DH), BF16),
        ],
        scratch_shapes=[pltpu.VMEM((heads, DH, DH), F32), pltpu.VMEM((heads, DH), F32)],
        compiler_params=pltpu.CompilerParams(vmem_limit_bytes=VMEM),
        cost_estimate=pl.CostEstimate(flops=1_000_000, bytes_accessed=1_000_000, transcendentals=0),
        name="delta_prep",
    )(log_decay, beta, delta_key, delta_query)


QB = 256
SCALE = 1.0 / math.sqrt(DH) * math.log2(math.e)


def own_kernel(q_ref, k_ref, v_ref, o_ref, vx):
    rows = q_ref.shape[0]
    vx[:, :DH] = v_ref[...]
    vx[:, DH:] = jnp.ones((rows, DH), BF16)
    ri = lax.broadcasted_iota(jnp.int32, (QB, QB), 0)
    rj = lax.broadcasted_iota(jnp.int32, (QB, QB), 1)
    lane = lax.broadcasted_iota(jnp.int32, (QB, DH), 1)
    blocks = [slice(i * QB, (i + 1) * QB) for i in range(rows // QB)]
    scores = []
    for here in blocks:
        s = dot(q_ref[here], k_ref[: here.stop], NT)
        edge = jnp.where(rj <= ri, s[:, here], NEG)
        scores.append(beside(s[:, : here.start], edge) if here.start else edge)
    for here, s in zip(blocks, scores):
        top = jnp.max(s, axis=1, keepdims=True)
        pv = dot(jnp.exp2((s - top) * SCALE).astype(BF16), vx[: here.stop])
        o_ref[here, :DH] = pv[:, :DH]
        o_ref[here, DH:] = jnp.where(lane < DH // 2, pv[:, DH:], top)


def own_part(att_query, att_key, att_value):
    rows, width = att_query.shape
    heads = width // DH
    tok = pl.BlockSpec((rows, DH), lambda h: (0, h))
    return pl.pallas_call(
        own_kernel,
        grid=(heads,),
        in_specs=[tok, tok, tok],
        out_specs=pl.BlockSpec((rows, 2 * DH), lambda h: (0, h)),
        out_shape=jax.ShapeDtypeStruct((rows, 2 * width), F32),
        scratch_shapes=[pltpu.VMEM((rows, 2 * DH), BF16)],
        compiler_params=pltpu.CompilerParams(vmem_limit_bytes=VMEM),
        cost_estimate=pl.CostEstimate(flops=100_000_000_000, bytes_accessed=1_000_000, transcendentals=0),
        name="own_attention",
    )(att_query, att_key, att_value)


def attend_kernel(
    first_ref, q_ref, kp_ref, ko_ref, vp_ref, own_ref, m_ref, ke_ref, qe_ref, e_ref, g_ref, r_ref, b_ref, kx, vx
):
    h = pl.program_id(0)
    first = first_ref[0]
    window = kp_ref.shape[0]
    vx[:, :DH] = vp_ref[...]

    @pl.when(first == 0)
    def _():
        kx[...] = kp_ref[...]
        vx[:, DH:] = jnp.ones((window, DH), BF16)

    @pl.when(first != 0)
    def _():
        kx[...] = jnp.broadcast_to(ko_ref[0:1].astype(F32), (window, DH)).astype(BF16)
        vx[:, DH:] = jnp.zeros((window, DH), BF16)

    ri = lax.broadcasted_iota(jnp.int32, (QB, QB), 0)
    rj = lax.broadcasted_iota(jnp.int32, (QB, QB), 1)
    mean = jnp.full((DH, DH), 1.0 / DH, BF16)
    blocks = [slice(i * QB, (i + 1) * QB) for i in range(q_ref.shape[0] // QB)]
    scores = []
    for i, here in enumerate(blocks):
        s = dot(q_ref[here], kx[i * QB :], NT)
        edge = jnp.where(rj > ri, s[:, :QB], NEG)
        scores.append(beside(edge, s[:, QB:]) if s.shape[1] > QB else edge)
    sums = []
    for i, (here, s) in enumerate(zip(blocks, scores)):
        own_top = own_ref[here, 2 * DH - 1 :]
        top = jnp.maximum(jnp.max(s, axis=1, keepdims=True), own_top)
        pv = dot(jnp.exp2((s - top) * SCALE).astype(BF16), vx[i * QB :])
        sums.append((pv, jnp.exp2((own_top - top) * SCALE)))
    outs = []
    for here, (pv, fade) in zip(blocks, sums):
        total = pv[:, DH:] + fade * own_ref[here, DH : DH + 1]
        outs.append(((pv[:, :DH] + fade * own_ref[here, :DH]) / total).astype(BF16).astype(F32))
    squares = [dot(beside(*halves(o * o)), below(mean, mean)) for o in outs]
    values = [halves(o * lax.rsqrt(square + 1e-6)) for o, square in zip(outs, squares)]
    per = QB // CHUNK
    chunks = []
    for c in range(m_ref.shape[0]):
        part = slice((c % per) * CHUNK, (c % per + 1) * CHUNK)
        chunks.append((values[c // per][0][part], values[c // per][1][part]))
    fresh = []
    for c, (vh, vl) in enumerate(chunks):
        ke = ke_ref[c, 0]
        fresh.append(dot(ke, below(vh, vh)) + dot(ke[:, :DH], vl))
    x = jnp.zeros((DH, DH), F32)
    states = []
    for c in range(len(chunks)):
        xh, xl = halves(x)
        states.append(below(xh, xl))
        x = g_ref[c, pl.ds(h, 1)] * x + dot(e_ref[c, 0], xh) + fresh[c]
    for c, (vh, vl) in enumerate(chunks):
        m, qe = m_ref[c, 0], qe_ref[c, 0]
        r_ref[c * CHUNK : (c + 1) * CHUNK] = dot(beside(m, m), below(vh, vl)) + dot(beside(qe, qe), states[c])
    b_ref[0] = jnp.transpose(x).astype(BF16)


def attend(first, att_query, k_prev, k_own, v_prev, own, m, ke, qe, e, g):
    rows, width = att_query.shape
    heads = width // DH
    window = k_prev.shape[0]
    chunks = rows // CHUNK
    big = pl.BlockSpec((chunks, 1, CHUNK, DH), lambda h: (0, h, 0, 0))
    tok = pl.BlockSpec((rows, DH), lambda h: (0, h))
    return pl.pallas_call(
        attend_kernel,
        grid=(heads,),
        in_specs=[
            pl.BlockSpec(memory_space=pltpu.SMEM),
            tok,
            pl.BlockSpec((window, DH), lambda h: (0, h)),
            pl.BlockSpec((16, DH), lambda h: (0, h)),
            pl.BlockSpec((window, DH), lambda h: (0, h)),
            pl.BlockSpec((rows, 2 * DH), lambda h: (0, h)),
            big,
            pl.BlockSpec((chunks, 1, CHUNK, 2 * DH), lambda h: (0, h, 0, 0)),
            big,
            big,
            pl.BlockSpec((chunks, heads, DH), lambda h: (0, 0, 0)),
        ],
        out_specs=[tok, pl.BlockSpec((1, DH, DH), lambda h: (h, 0, 0))],
        out_shape=[
            jax.ShapeDtypeStruct((rows, width), F32),
            jax.ShapeDtypeStruct((heads, DH, DH), BF16),
        ],
        scratch_shapes=[pltpu.VMEM((window, DH), BF16), pltpu.VMEM((window, 2 * DH), BF16)],
        compiler_params=pltpu.CompilerParams(vmem_limit_bytes=MIDDLE),
        cost_estimate=pl.CostEstimate(flops=100_000_000_000, bytes_accessed=1_000_000, transcendentals=0),
        name="window_attention",
    )(first, att_query, k_prev, k_own, v_prev, own, m, ke, qe, e, g)


def vmem_call(kernel, outs, name, *args):
    vm = pl.BlockSpec(memory_space=pltpu.VMEM)
    return pl.pallas_call(
        kernel,
        in_specs=[vm] * len(args),
        out_specs=[vm] * len(outs),
        out_shape=[jax.ShapeDtypeStruct(*o) for o in outs],
        compiler_params=pltpu.CompilerParams(vmem_limit_bytes=SMALL),
        cost_estimate=pl.CostEstimate(flops=1_000_000, bytes_accessed=1_000_000, transcendentals=0),
        name=name,
    )(*args)


def follow(g, f, d_ref):
    d = d_ref[:DH]
    step = unpack_gain(d_ref[DH:])
    return g * step, step * f + g * d.astype(F32) + dot(f.astype(BF16), d)


def prefix_kernel(d_ref, p_ref, t_ref):
    g = jnp.ones((1, DH), F32)
    f = jnp.zeros((DH, DH), F32)
    count = d_ref.shape[0]
    for z in range(count):
        p_ref[z, :DH] = f.astype(BF16)
        p_ref[z, DH:] = pack_gain(g)
        g, f = follow(g, f, d_ref.at[z])
    t_ref[:DH] = f.astype(BF16)
    t_ref[DH:] = pack_gain(g)


def line_kernel(d_ref, b_ref, q_ref, t_ref):
    acc = b_ref[0].astype(F32)
    q_ref[0] = jnp.zeros_like(acc)
    for z in range(1, d_ref.shape[0]):
        q_ref[z] = acc
        g = unpack_gain(d_ref[z, DH:])
        acc = g * acc + b_ref[z].astype(F32) + dot(acc.astype(BF16), d_ref[z, :DH])
    t_ref[...] = acc


def place_kernel(majors, *refs):
    sums, fades = refs[: majors - 1], refs[majors - 1 : 2 * majors - 3]
    p_ref, q_ref, s_ref = refs[2 * majors - 3 :]
    base = sums[0][...]
    g = jnp.ones((1, DH), F32)
    f = jnp.zeros((DH, DH), F32)
    for k in range(1, majors - 1):
        d = fades[k - 1]
        step = unpack_gain(d[DH:])
        if k == 1:
            g, f = step, d[:DH].astype(F32)
        else:
            old = d[:DH]
            f, g = step * f + g * old.astype(F32) + dot(old, f.astype(BF16)), g * step
        value = sums[k][...]
        base = base + g * value + dot(value.astype(BF16), f.astype(BF16))
    high = base.astype(BF16)
    for z in range(p_ref.shape[0]):
        out = unpack_gain(p_ref[z, DH:]) * base + q_ref[z] + dot(high, p_ref[z, :DH])
        s_ref[z] = out.astype(BF16)


def finish_kernel(heads, r_ref, qf_ref, s_ref, gate_ref, gain_ref, o_ref):
    gain = gain_ref[...]
    mean = jnp.full((DH, DH), 1.0 / DH, BF16)
    tiles = [
        (slice(c * CHUNK, (c + 1) * CHUNK), slice(h * DH, (h + 1) * DH), c, h)
        for c in range(qf_ref.shape[0])
        for h in range(heads)
    ]
    reads = [r_ref[rows, cols] + dot(qf_ref[c, h], beside(s_ref[h], s_ref[h]), NT) for rows, cols, c, h in tiles]
    squares = [dot(beside(*halves(r * r)), below(mean, mean)) for r in reads]
    for (rows, cols, c, h), r, square in zip(tiles, reads, squares):
        gate = gate_ref[rows, cols].astype(F32)
        r = r * lax.rsqrt(square + 1e-6) * gain
        o_ref[rows, cols] = (r * (gate / (1.0 + jnp.exp(-gate)))).astype(BF16)


def finish(readout, qf, state, out_gate, gain):
    rows, width = readout.shape
    heads = width // DH
    tok = pl.BlockSpec((PER * CHUNK, width), lambda c: (c, 0))
    return pl.pallas_call(
        functools.partial(finish_kernel, heads),
        grid=(rows // (PER * CHUNK),),
        in_specs=[
            tok,
            pl.BlockSpec((PER, heads, CHUNK, 2 * DH), lambda c: (c, 0, 0, 0)),
            pl.BlockSpec((heads, DH, DH), lambda c: (0, 0, 0)),
            tok,
            pl.BlockSpec((1, DH), lambda c: (0, 0)),
        ],
        out_specs=tok,
        out_shape=jax.ShapeDtypeStruct((rows, width), BF16),
        compiler_params=pltpu.CompilerParams(vmem_limit_bytes=VMEM),
        cost_estimate=pl.CostEstimate(flops=140_000_000, bytes_accessed=6_000_000, transcendentals=600_000),
        name="gated_readout",
    )(readout, qf, state, out_gate, gain)


def body(att_query, att_key, att_value, delta_query, delta_key, out_gate, log_decay, beta, norm_gain):
    heads = log_decay.shape[0]
    count = lax.axis_size("seq")
    minor = 2 * heads
    majors = count // minor
    place = lax.axis_index("seq")
    onward = [(s, s + 1) for s in range(count - 1)]
    k_prev = lax.ppermute(att_key, "seq", onward)
    v_prev = lax.ppermute(att_value, "seq", onward)
    copies = minor // heads
    m, ke, qe, qf, e, g, wire = prep(log_decay, beta, delta_key, delta_query, copies)
    own = own_part(att_query, att_key, att_value)
    lines = [[x * minor + z for z in range(minor)] for x in range(majors)]
    d_line = lax.all_to_all(wire, "seq", 0, 0, axis_index_groups=lines)
    first = jnp.reshape((place == 0).astype(jnp.int32), (1,))
    readout, b = attend(first, att_query, k_prev, att_key, v_prev, own, m, ke, qe, e, g)
    d_line, b = lax.optimization_barrier((d_line, b))
    p_line, d_total = vmem_call(
        prefix_kernel, [(d_line.shape, BF16), (d_line.shape[1:], BF16)], "decay_prefix", d_line
    )

    def from_lines(value, back):
        hops = back * minor
        return lax.ppermute(value, "seq", [(s, s + hops) for s in range(count - hops)])

    fades = [from_lines(d_total, k) for k in range(1, majors - 1)]
    b, p_line = lax.optimization_barrier((b, p_line))
    size = DH // copies
    b_line = lax.all_to_all(b.reshape(minor, size, DH), "seq", 0, 0, axis_index_groups=lines)
    q_line, b_total = vmem_call(
        line_kernel, [(b_line.shape, F32), ((size, DH), F32)], "line_states", d_line, b_line
    )
    sums = [from_lines(b_total, k) for k in range(1, majors)]
    (s_line,) = vmem_call(
        functools.partial(place_kernel, majors), [(b_line.shape, BF16)], "block_states", *sums, *fades, p_line, q_line
    )
    state = lax.all_to_all(s_line, "seq", 0, 0, axis_index_groups=lines).reshape(heads, DH, DH)
    return finish(readout, qf, state, out_gate, norm_gain.reshape(1, DH))


def solution(mesh):
    tokens = P(("doc", "seq"), "head")
    gates = P("head", ("doc", "seq"))
    return jax.shard_map(
        body,
        mesh=mesh,
        in_specs=(tokens,) * 6 + (gates, gates, P()),
        out_specs=tokens,
        check_vma=False,
    )
```

```python
import functools
import math

import jax
import jax.numpy as jnp
from jax import lax
from jax.experimental import pallas as pl
from jax.experimental.pallas import tpu as pltpu
from jax.sharding import PartitionSpec as P

CHUNK = 128
DH = 128
WIRE = 144
VMEM = 60 * 2**20
MIDDLE = 58 * 2**20
SMALL = 8 * 2**20
NEG = -1e30
F32 = jnp.float32
BF16 = jnp.bfloat16
NN = (((1,), (0,)), ((), ()))
NT = (((1,), (1,)), ((), ()))


def dot(a, b, dims=NN):
    return lax.dot_general(a, b, dims, preferred_element_type=F32)


def shift_lanes(row, steps):
    lane = lax.broadcasted_iota(jnp.int32, row.shape, 1)
    return jnp.where(lane >= steps, pltpu.roll(row, steps, axis=1), 0.0)


def halves(value):
    high = value.astype(BF16)
    return high, (value - high.astype(F32)).astype(BF16)


def beside(*parts):
    return jnp.concatenate(parts, axis=1)


def below(*parts):
    return jnp.concatenate(parts, axis=0)


def diagonal(one, two):
    return below(beside(one, jnp.zeros_like(two)), beside(jnp.zeros_like(one), two))


def odd_rows(value, size):
    return below(*[value[i : i + size] for i in range(size, value.shape[0], 2 * size)])


def less_odd_rows(value, change, size):
    parts = []
    for n, i in enumerate(range(0, value.shape[0], 2 * size)):
        parts += [value[i : i + size], value[i + size : i + 2 * size] - change[n * size : (n + 1) * size]]
    return below(*parts)


def split_three(g):
    high = g.astype(BF16)
    rest = g - high.astype(F32)
    mid = rest.astype(BF16)
    low = (rest - mid.astype(F32)).astype(BF16)
    return high, mid, low


def pack_gain(g):
    row = lax.broadcasted_iota(jnp.int32, (WIRE - DH, DH), 0)
    high, mid, low = split_three(g)
    block = jnp.where(
        row == 0,
        high.astype(F32),
        jnp.where(row == 1, mid.astype(F32), jnp.where(row == 2, low.astype(F32), 0.0)),
    )
    return block.astype(BF16)


def unpack_gain(block):
    rows = block.astype(F32)
    return rows[0:1] + rows[1:2] + rows[2:3]


def gate_rows(heads, ld, be):
    rows = below(ld, be)
    cum = rows
    for steps in (1, 2, 4, 8, 16, 32, 64):
        cum = cum + shift_lanes(cum, steps)
    row8 = lax.broadcasted_iota(jnp.int32, (2 * heads, CHUNK), 0)
    return jnp.where(row8 < heads, cum, rows)


def prep_kernel(
    heads, per, ld_ref, be_ref, k_ref, q_ref, m_ref, ke_ref, qe_ref, qf_ref, e_ref, g_ref, w_ref, f_scr, gp_scr
):
    step = pl.program_id(0)

    @pl.when(step == 0)
    def _():
        f_scr[...] = jnp.zeros_like(f_scr)
        gp_scr[...] = jnp.ones_like(gp_scr)

    ti = lax.broadcasted_iota(jnp.int32, (CHUNK, CHUNK), 0)
    tj = lax.broadcasted_iota(jnp.int32, (CHUNK, CHUNK), 1)
    eye = jnp.where(ti == tj, 1.0, 0.0)
    state = []
    ts = []
    products = []
    diags = []
    for c in range(per):
        part = slice(c * CHUNK, (c + 1) * CHUNK)
        rows = gate_rows(heads, ld_ref[:, part], be_ref[:, part])
        cols = jnp.transpose(rows)
        keys = []
        colmat = jnp.zeros((CHUNK, CHUNK), F32)
        for h in range(heads):
            k = k_ref[part, h * DH : (h + 1) * DH]
            kf = k.astype(F32)
            rk = lax.rsqrt(jnp.sum(kf * kf, axis=1, keepdims=True) + 1e-6)
            keys.append((k, kf, rk))
            colmat = jnp.where(tj == h, rk, colmat)
        rowmat = jnp.transpose(colmat)
        for h in range(0, heads, 2):
            two = slice(h * DH, (h + 2) * DH)
            kd = diagonal(keys[h][0], keys[h + 1][0])
            diags.append(kd)
            kk2 = dot(k_ref[part, two], kd, NT)
            qk2 = dot(q_ref[part, two], kd, NT)
            products.append((kk2[:, :CHUNK], qk2[:, :CHUNK]))
            products.append((kk2[:, CHUNK:], qk2[:, CHUNK:]))
        for h in range(heads):
            k, kf, rk_c = keys[h]
            kk, qk = products[c * heads + h]
            rk_r = rowmat[h : h + 1]
            qf = q_ref[part, h * DH : (h + 1) * DH].astype(F32)
            rq_c = lax.rsqrt(jnp.sum(qf * qf, axis=1, keepdims=True) + 1e-6)
            g_c = cols[:, h : h + 1]
            g_r = rows[h : h + 1]
            b_c = cols[:, heads + h : heads + h + 1]
            b_r = rows[heads + h : heads + h + 1]
            decay = jnp.exp(jnp.where(ti >= tj, g_c - g_r, NEG)) * rk_r
            a = beside(*halves(decay * rq_c * qk))
            low = jnp.where(ti > tj, decay * (b_c * rk_c) * kk, 0.0)
            ts.append(eye - jnp.where((ti >> 1) == (tj >> 1), low, 0.0))
            state.append((kf, rk_c, rk_r, qf, rq_c, g_c, g_r, b_r, a, low))
    count = per * heads
    for shift in range(1, 7):
        pair = (ti >> (shift + 1)) == (tj >> (shift + 1))
        cross = pair & (((ti >> shift) & 1) == 1) & (((tj >> shift) & 1) == 0)
        size = 1 << shift
        tb = [t.astype(BF16) for t in ts]
        lead = [odd_rows(t, size).astype(BF16) for t in ts] if size >= 8 else tb
        lm = [below(*halves(jnp.where(cross, s[-1], 0.0))) for s in state]
        mid = [dot(beside(x, x), y).astype(BF16) for x, y in zip(lead, lm)]
        change = []
        for n in range(0, count, 2):
            both = dot(beside(mid[n], mid[n + 1]), diagonal(tb[n], tb[n + 1]))
            change += [both[:, :CHUNK], both[:, CHUNK:]]
        if size >= 8:
            ts = [less_odd_rows(t, x, size) for t, x in zip(ts, change)]
        else:
            ts = [t - x for t, x in zip(ts, change)]
    ws = []
    for n in range(0, count, 2):
        lead = []
        for s, t in zip(state[n : n + 2], ts[n : n + 2]):
            lead.append((t * (s[7] * jnp.exp(s[6]) * s[2])).astype(BF16))
        both = dot(beside(*lead), diags[n // 2])
        ws += [both[:, :DH], both[:, DH:]]
    starts = []
    for n in range(count):
        c, h = n // heads, n % heads
        kf, rk_c, rk_r, qf, rq_c, g_c, g_r, b_r, a, low = state[n]
        t, w = ts[n], ws[n]
        tail_c = jnp.exp(g_r[:, CHUNK - 1 : CHUNK] - g_c) * rk_c
        tw = beside(t.astype(BF16), w.astype(BF16))
        both = dot(a, below(tw, tw))
        m_ref[c, h] = (both[:, :CHUNK] * b_r).astype(BF16)
        qe = (jnp.exp(g_c) * rq_c) * qf - both[:, CHUNK:]
        kt = jnp.transpose(kf).astype(BF16)
        th, tl = halves(tail_c * t * b_r)
        wh, wl = halves(tail_c * w)
        both = dot(beside(kt, kt), below(beside(th, wh), beside(tl, wl)))
        ke_ref[c, h] = beside(*halves(both[:, :CHUNK]))
        e = -both[:, CHUNK:]
        qeb, eb = qe.astype(BF16), e.astype(BF16)
        qe_ref[c, h] = qeb
        e_ref[c, h] = eb
        starts.append((qe, e, below(qeb, eb), jnp.broadcast_to(jnp.exp(g_r[:, CHUNK - 1 : CHUNK]), (1, DH))))
    for c in range(per):
        for h in range(0, heads, 2):
            ones = starts[c * heads + h : c * heads + h + 2]
            fs = [f_scr[h], f_scr[h + 1]]
            both = dot(beside(ones[0][2], ones[1][2]), diagonal(fs[0].astype(BF16), fs[1].astype(BF16)))
            for n, (qe, e, _, gc) in enumerate(ones):
                part = both[:, n * DH : (n + 1) * DH]
                gp = gp_scr[h + n : h + n + 1]
                qf_ref[c, h + n] = beside(*halves(gp * qe + part[:CHUNK]))
                f_scr[h + n] = gc * fs[n] + gp * e + part[CHUNK:]
                gp_scr[h + n : h + n + 1] = gp * gc
                g_ref[c, h + n : h + n + 1] = gc

    @pl.when(step == pl.num_programs(0) - 1)
    def _():
        for h in range(heads):
            matrix = jnp.transpose(f_scr[h]).astype(BF16)
            gain = pack_gain(gp_scr[h : h + 1])
            for copy in range(w_ref.shape[0] // heads):
                w_ref[h * (w_ref.shape[0] // heads) + copy, :DH] = matrix
                w_ref[h * (w_ref.shape[0] // heads) + copy, DH:] = gain


PER = 4


def prep(log_decay, beta, delta_key, delta_query, copies):
    heads, rows = log_decay.shape
    chunks = rows // CHUNK
    big = jax.ShapeDtypeStruct((chunks, heads, CHUNK, DH), BF16)
    wide = jax.ShapeDtypeStruct((chunks, heads, CHUNK, 2 * DH), BF16)
    big_spec = pl.BlockSpec((PER, heads, CHUNK, DH), lambda c: (c, 0, 0, 0))
    wide_spec = pl.BlockSpec((PER, heads, CHUNK, 2 * DH), lambda c: (c, 0, 0, 0))
    row_spec = pl.BlockSpec((heads, PER * CHUNK), lambda c: (0, c))
    tok_spec = pl.BlockSpec((PER * CHUNK, heads * DH), lambda c: (c, 0))
    return pl.pallas_call(
        functools.partial(prep_kernel, heads, PER),
        grid=(chunks // PER,),
        in_specs=[row_spec, row_spec, tok_spec, tok_spec],
        out_specs=[big_spec, wide_spec, big_spec, wide_spec, big_spec]
        + [
            pl.BlockSpec((PER, heads, DH), lambda c: (c, 0, 0)),
            pl.BlockSpec((heads * copies, WIRE, DH), lambda c: (0, 0, 0)),
        ],
        out_shape=[big, wide, big, wide, big]
        + [
            jax.ShapeDtypeStruct((chunks, heads, DH), F32),
            jax.ShapeDtypeStruct((heads * copies, WIRE, DH), BF16),
        ],
        scratch_shapes=[pltpu.VMEM((heads, DH, DH), F32), pltpu.VMEM((heads, DH), F32)],
        compiler_params=pltpu.CompilerParams(vmem_limit_bytes=VMEM),
        cost_estimate=pl.CostEstimate(flops=1_000_000, bytes_accessed=1_000_000, transcendentals=0),
        name="delta_prep",
    )(log_decay, beta, delta_key, delta_query)


QB = 256
SCALE = 1.0 / math.sqrt(DH) * math.log2(math.e)


def own_kernel(q_ref, k_ref, v_ref, o_ref, vx):
    rows = q_ref.shape[0]
    vx[:, :DH] = v_ref[...]
    vx[:, DH:] = jnp.ones((rows, DH), BF16)
    ri = lax.broadcasted_iota(jnp.int32, (QB, QB), 0)
    rj = lax.broadcasted_iota(jnp.int32, (QB, QB), 1)
    lane = lax.broadcasted_iota(jnp.int32, (QB, DH), 1)
    blocks = [slice(i * QB, (i + 1) * QB) for i in range(rows // QB)]
    scores = []
    for here in blocks:
        s = dot(q_ref[here], k_ref[: here.stop], NT)
        edge = jnp.where(rj <= ri, s[:, here], NEG)
        scores.append(beside(s[:, : here.start], edge) if here.start else edge)
    for here, s in zip(blocks, scores):
        top = jnp.max(s, axis=1, keepdims=True)
        pv = dot(jnp.exp2((s - top) * SCALE).astype(BF16), vx[: here.stop])
        o_ref[here, :DH] = pv[:, :DH]
        o_ref[here, DH:] = jnp.where(lane < DH // 2, pv[:, DH:], top)


def own_part(att_query, att_key, att_value):
    rows, width = att_query.shape
    heads = width // DH
    tok = pl.BlockSpec((rows, DH), lambda h: (0, h))
    return pl.pallas_call(
        own_kernel,
        grid=(heads,),
        in_specs=[tok, tok, tok],
        out_specs=pl.BlockSpec((rows, 2 * DH), lambda h: (0, h)),
        out_shape=jax.ShapeDtypeStruct((rows, 2 * width), F32),
        scratch_shapes=[pltpu.VMEM((rows, 2 * DH), BF16)],
        compiler_params=pltpu.CompilerParams(vmem_limit_bytes=VMEM),
        cost_estimate=pl.CostEstimate(flops=100_000_000_000, bytes_accessed=1_000_000, transcendentals=0),
        name="own_attention",
    )(att_query, att_key, att_value)


def attend_kernel(
    base, first_ref, q_ref, kp_ref, ko_ref, vp_ref, own_ref, m_ref, ke_ref, qe_ref, e_ref, g_ref, *rest
):
    r_ref, b_ref, kx, vx = rest[-4:]
    h = pl.program_id(0) + base
    first = first_ref[0]
    window = kp_ref.shape[0]
    vx[:, :DH] = vp_ref[...]

    @pl.when(first == 0)
    def _():
        kx[...] = kp_ref[...]
        vx[:, DH:] = jnp.ones((window, DH), BF16)

    @pl.when(first != 0)
    def _():
        kx[...] = jnp.broadcast_to(ko_ref[0:1].astype(F32), (window, DH)).astype(BF16)
        vx[:, DH:] = jnp.zeros((window, DH), BF16)

    ri = lax.broadcasted_iota(jnp.int32, (QB, QB), 0)
    rj = lax.broadcasted_iota(jnp.int32, (QB, QB), 1)
    mean = jnp.full((DH, DH), 1.0 / DH, BF16)
    blocks = [slice(i * QB, (i + 1) * QB) for i in range(q_ref.shape[0] // QB)]
    scores = []
    for i, here in enumerate(blocks):
        s = dot(q_ref[here], kx[i * QB :], NT)
        edge = jnp.where(rj > ri, s[:, :QB], NEG)
        scores.append(beside(edge, s[:, QB:]) if s.shape[1] > QB else edge)
    sums = []
    for i, (here, s) in enumerate(zip(blocks, scores)):
        own_top = own_ref[here, 2 * DH - 1 :]
        top = jnp.maximum(jnp.max(s, axis=1, keepdims=True), own_top)
        pv = dot(jnp.exp2((s - top) * SCALE).astype(BF16), vx[i * QB :])
        sums.append((pv, jnp.exp2((own_top - top) * SCALE)))
    outs = []
    for here, (pv, fade) in zip(blocks, sums):
        total = pv[:, DH:] + fade * own_ref[here, DH : DH + 1]
        outs.append(((pv[:, :DH] + fade * own_ref[here, :DH]) / total).astype(BF16).astype(F32))
    squares = [dot(beside(*halves(o * o)), below(mean, mean)) for o in outs]
    values = [halves(o * lax.rsqrt(square + 1e-6)) for o, square in zip(outs, squares)]
    per = QB // CHUNK
    chunks = []
    for c in range(m_ref.shape[0]):
        part = slice((c % per) * CHUNK, (c % per + 1) * CHUNK)
        chunks.append((values[c // per][0][part], values[c // per][1][part]))
    fresh = []
    for c, (vh, vl) in enumerate(chunks):
        ke = ke_ref[c, 0]
        fresh.append(dot(ke, below(vh, vh)) + dot(ke[:, :DH], vl))
    x = jnp.zeros((DH, DH), F32)
    states = []
    for c in range(len(chunks)):
        xh, xl = halves(x)
        states.append(below(xh, xl))
        x = g_ref[c, pl.ds(h, 1)] * x + dot(e_ref[c, 0], xh) + fresh[c]
    for c, (vh, vl) in enumerate(chunks):
        m, qe = m_ref[c, 0], qe_ref[c, 0]
        r_ref[c * CHUNK : (c + 1) * CHUNK] = dot(beside(m, m), below(vh, vl)) + dot(beside(qe, qe), states[c])
    b_ref[0] = jnp.transpose(x).astype(BF16)


def attend(base, first, att_query, k_prev, k_own, v_prev, own, m, ke, qe, e, g, *earlier):
    rows, width = att_query.shape
    heads = width // DH
    window, held = k_prev.shape
    chunks = rows // CHUNK
    big = pl.BlockSpec((chunks, 1, CHUNK, DH), lambda h: (0, h + base, 0, 0))
    tok = pl.BlockSpec((rows, DH), lambda h: (0, h + base))
    prev = pl.BlockSpec((window, DH), lambda h: (0, h))
    return pl.pallas_call(
        functools.partial(attend_kernel, base),
        grid=(held // DH,),
        in_specs=[
            pl.BlockSpec(memory_space=pltpu.SMEM),
            tok,
            prev,
            pl.BlockSpec((16, DH), lambda h: (0, h + base)),
            prev,
            pl.BlockSpec((rows, 2 * DH), lambda h: (0, h + base)),
            big,
            pl.BlockSpec((chunks, 1, CHUNK, 2 * DH), lambda h: (0, h + base, 0, 0)),
            big,
            big,
            pl.BlockSpec((chunks, heads, DH), lambda h: (0, 0, 0)),
        ]
        + [pl.BlockSpec(memory_space=pl.ANY)] * len(earlier),
        out_specs=[tok, pl.BlockSpec((1, DH, DH), lambda h: (h + base, 0, 0))],
        out_shape=[
            jax.ShapeDtypeStruct((rows, width), F32),
            jax.ShapeDtypeStruct((heads, DH, DH), BF16),
        ],
        input_output_aliases={11 + n: n for n in range(len(earlier))},
        scratch_shapes=[pltpu.VMEM((window, DH), BF16), pltpu.VMEM((window, 2 * DH), BF16)],
        compiler_params=pltpu.CompilerParams(vmem_limit_bytes=MIDDLE),
        cost_estimate=pl.CostEstimate(flops=100_000_000_000, bytes_accessed=1_000_000, transcendentals=0),
        name="window_attention",
    )(first, att_query, k_prev, k_own, v_prev, own, m, ke, qe, e, g, *earlier)


def vmem_call(kernel, outs, name, *args):
    vm = pl.BlockSpec(memory_space=pltpu.VMEM)
    return pl.pallas_call(
        kernel,
        in_specs=[vm] * len(args),
        out_specs=[vm] * len(outs),
        out_shape=[jax.ShapeDtypeStruct(*o) for o in outs],
        compiler_params=pltpu.CompilerParams(vmem_limit_bytes=SMALL),
        cost_estimate=pl.CostEstimate(flops=1_000_000, bytes_accessed=1_000_000, transcendentals=0),
        name=name,
    )(*args)


def follow(g, f, d_ref):
    d = d_ref[:DH]
    step = unpack_gain(d_ref[DH:])
    return g * step, step * f + g * d.astype(F32) + dot(f.astype(BF16), d)


def prefix_kernel(d_ref, p_ref, t_ref):
    g = jnp.ones((1, DH), F32)
    f = jnp.zeros((DH, DH), F32)
    count = d_ref.shape[0]
    for z in range(count):
        p_ref[z, :DH] = f.astype(BF16)
        p_ref[z, DH:] = pack_gain(g)
        g, f = follow(g, f, d_ref.at[z])
    t_ref[:DH] = f.astype(BF16)
    t_ref[DH:] = pack_gain(g)


def line_kernel(d_ref, b_ref, q_ref, t_ref):
    acc = b_ref[0].astype(F32)
    q_ref[0] = jnp.zeros_like(acc)
    for z in range(1, d_ref.shape[0]):
        q_ref[z] = acc
        g = unpack_gain(d_ref[z, DH:])
        acc = g * acc + b_ref[z].astype(F32) + dot(acc.astype(BF16), d_ref[z, :DH])
    t_ref[...] = acc


def place_kernel(majors, *refs):
    sums, fades = refs[: majors - 1], refs[majors - 1 : 2 * majors - 3]
    p_ref, q_ref, s_ref = refs[2 * majors - 3 :]
    base = sums[0][...]
    g = jnp.ones((1, DH), F32)
    f = jnp.zeros((DH, DH), F32)
    for k in range(1, majors - 1):
        d = fades[k - 1]
        step = unpack_gain(d[DH:])
        if k == 1:
            g, f = step, d[:DH].astype(F32)
        else:
            old = d[:DH]
            f, g = step * f + g * old.astype(F32) + dot(old, f.astype(BF16)), g * step
        value = sums[k][...]
        base = base + g * value + dot(value.astype(BF16), f.astype(BF16))
    high = base.astype(BF16)
    for z in range(p_ref.shape[0]):
        out = unpack_gain(p_ref[z, DH:]) * base + q_ref[z] + dot(high, p_ref[z, :DH])
        s_ref[z] = out.astype(BF16)


def finish_kernel(heads, r_ref, qf_ref, s_ref, gate_ref, gain_ref, o_ref):
    gain = gain_ref[...]
    mean = jnp.full((DH, DH), 1.0 / DH, BF16)
    tiles = [
        (slice(c * CHUNK, (c + 1) * CHUNK), slice(h * DH, (h + 1) * DH), c, h)
        for c in range(qf_ref.shape[0])
        for h in range(heads)
    ]
    reads = [r_ref[rows, cols] + dot(qf_ref[c, h], beside(s_ref[h], s_ref[h]), NT) for rows, cols, c, h in tiles]
    squares = [dot(beside(*halves(r * r)), below(mean, mean)) for r in reads]
    for (rows, cols, c, h), r, square in zip(tiles, reads, squares):
        gate = gate_ref[rows, cols].astype(F32)
        r = r * lax.rsqrt(square + 1e-6) * gain
        o_ref[rows, cols] = (r * (gate / (1.0 + jnp.exp(-gate)))).astype(BF16)


def finish(readout, qf, state, out_gate, gain):
    rows, width = readout.shape
    heads = width // DH
    tok = pl.BlockSpec((PER * CHUNK, width), lambda c: (c, 0))
    return pl.pallas_call(
        functools.partial(finish_kernel, heads),
        grid=(rows // (PER * CHUNK),),
        in_specs=[
            tok,
            pl.BlockSpec((PER, heads, CHUNK, 2 * DH), lambda c: (c, 0, 0, 0)),
            pl.BlockSpec((heads, DH, DH), lambda c: (0, 0, 0)),
            tok,
            pl.BlockSpec((1, DH), lambda c: (0, 0)),
        ],
        out_specs=tok,
        out_shape=jax.ShapeDtypeStruct((rows, width), BF16),
        compiler_params=pltpu.CompilerParams(vmem_limit_bytes=VMEM),
        cost_estimate=pl.CostEstimate(flops=140_000_000, bytes_accessed=6_000_000, transcendentals=600_000),
        name="gated_readout",
    )(readout, qf, state, out_gate, gain)


def body(att_query, att_key, att_value, delta_query, delta_key, out_gate, log_decay, beta, norm_gain):
    heads = log_decay.shape[0]
    count = lax.axis_size("seq")
    minor = 2 * heads
    majors = count // minor
    place = lax.axis_index("seq")
    onward = [(s, s + 1) for s in range(count - 1)]
    half = heads // 2 * DH
    k_first = lax.ppermute(att_key[:, :half], "seq", onward)
    v_first = lax.ppermute(att_value[:, :half], "seq", onward)
    copies = minor // heads
    m, ke, qe, qf, e, g, wire = prep(log_decay, beta, delta_key, delta_query, copies)
    wire, k_rest, v_rest = lax.optimization_barrier((wire, att_key[:, half:], att_value[:, half:]))
    lines = [[x * minor + z for z in range(minor)] for x in range(majors)]
    d_line = lax.all_to_all(wire, "seq", 0, 0, axis_index_groups=lines)
    k_rest = lax.ppermute(k_rest, "seq", onward)
    v_rest = lax.ppermute(v_rest, "seq", onward)
    own = own_part(att_query, att_key, att_value)
    d_line, own = lax.optimization_barrier((d_line, own))
    p_line, d_total = vmem_call(
        prefix_kernel, [(d_line.shape, BF16), (d_line.shape[1:], BF16)], "decay_prefix", d_line
    )

    def from_lines(value, back):
        hops = back * minor
        return lax.ppermute(value, "seq", [(s, s + hops) for s in range(count - hops)])

    fades = [from_lines(d_total, k) for k in range(1, majors - 1)]
    own, p_line = lax.optimization_barrier((own, p_line))
    first = jnp.reshape((place == 0).astype(jnp.int32), (1,))
    coefs = (own, m, ke, qe, e, g)
    early = attend(0, first, att_query, k_first, att_key, v_first, *coefs)
    early, fades = lax.optimization_barrier((early, fades))
    readout, b = attend(half // DH, first, att_query, k_rest, att_key, v_rest, *coefs, *early)
    size = DH // copies
    b_line = lax.all_to_all(b.reshape(minor, size, DH), "seq", 0, 0, axis_index_groups=lines)
    q_line, b_total = vmem_call(
        line_kernel, [(b_line.shape, F32), ((size, DH), F32)], "line_states", d_line, b_line
    )
    sums = [from_lines(b_total, k) for k in range(1, majors)]
    (s_line,) = vmem_call(
        functools.partial(place_kernel, majors), [(b_line.shape, BF16)], "block_states", *sums, *fades, p_line, q_line
    )
    state = lax.all_to_all(s_line, "seq", 0, 0, axis_index_groups=lines).reshape(heads, DH, DH)
    return finish(readout, qf, state, out_gate, norm_gain.reshape(1, DH))


def solution(mesh):
    tokens = P(("doc", "seq"), "head")
    gates = P("head", ("doc", "seq"))
    return jax.shard_map(
        body,
        mesh=mesh,
        in_specs=(tokens,) * 6 + (gates, gates, P()),
        out_specs=tokens,
        check_vma=False,
    )
```

```python
import functools
import math

import jax
import jax.numpy as jnp
from jax import lax
from jax.experimental import pallas as pl
from jax.experimental.pallas import tpu as pltpu
from jax.sharding import PartitionSpec as P

CHUNK = 128
DH = 128
WIRE = 144
VMEM = 60 * 2**20
MIDDLE = 58 * 2**20
SMALL = 8 * 2**20
NEG = -1e30
F32 = jnp.float32
BF16 = jnp.bfloat16
NN = (((1,), (0,)), ((), ()))
NT = (((1,), (1,)), ((), ()))


def dot(a, b, dims=NN):
    return lax.dot_general(a, b, dims, preferred_element_type=F32)


def shift_lanes(row, steps):
    lane = lax.broadcasted_iota(jnp.int32, row.shape, 1)
    return jnp.where(lane >= steps, pltpu.roll(row, steps, axis=1), 0.0)


def halves(value):
    high = value.astype(BF16)
    return high, (value - high.astype(F32)).astype(BF16)


def beside(*parts):
    return jnp.concatenate(parts, axis=1)


def below(*parts):
    return jnp.concatenate(parts, axis=0)


def diagonal(one, two):
    return below(beside(one, jnp.zeros_like(two)), beside(jnp.zeros_like(one), two))


def odd_rows(value, size):
    return below(*[value[i : i + size] for i in range(size, value.shape[0], 2 * size)])


def less_odd_rows(value, change, size):
    parts = []
    for n, i in enumerate(range(0, value.shape[0], 2 * size)):
        parts += [value[i : i + size], value[i + size : i + 2 * size] - change[n * size : (n + 1) * size]]
    return below(*parts)


def split_three(g):
    high = g.astype(BF16)
    rest = g - high.astype(F32)
    mid = rest.astype(BF16)
    low = (rest - mid.astype(F32)).astype(BF16)
    return high, mid, low


def pack_gain(g):
    row = lax.broadcasted_iota(jnp.int32, (WIRE - DH, DH), 0)
    high, mid, low = split_three(g)
    block = jnp.where(
        row == 0,
        high.astype(F32),
        jnp.where(row == 1, mid.astype(F32), jnp.where(row == 2, low.astype(F32), 0.0)),
    )
    return block.astype(BF16)


def unpack_gain(block):
    rows = block.astype(F32)
    return rows[0:1] + rows[1:2] + rows[2:3]


def gate_rows(heads, ld, be):
    rows = below(ld, be)
    cum = rows
    for steps in (1, 2, 4, 8, 16, 32, 64):
        cum = cum + shift_lanes(cum, steps)
    row8 = lax.broadcasted_iota(jnp.int32, (2 * heads, CHUNK), 0)
    return jnp.where(row8 < heads, cum, rows)


def prep_kernel(
    heads, per, ld_ref, be_ref, k_ref, q_ref, m_ref, ke_ref, qe_ref, qf_ref, e_ref, g_ref, w_ref, f_scr, gp_scr
):
    step = pl.program_id(0)

    @pl.when(step == 0)
    def _():
        f_scr[...] = jnp.zeros_like(f_scr)
        gp_scr[...] = jnp.ones_like(gp_scr)

    ti = lax.broadcasted_iota(jnp.int32, (CHUNK, CHUNK), 0)
    tj = lax.broadcasted_iota(jnp.int32, (CHUNK, CHUNK), 1)
    eye = jnp.where(ti == tj, 1.0, 0.0)
    state = []
    ts = []
    products = []
    diags = []
    for c in range(per):
        part = slice(c * CHUNK, (c + 1) * CHUNK)
        rows = gate_rows(heads, ld_ref[:, part], be_ref[:, part])
        cols = jnp.transpose(rows)
        keys = []
        colmat = jnp.zeros((CHUNK, CHUNK), F32)
        for h in range(heads):
            k = k_ref[part, h * DH : (h + 1) * DH]
            kf = k.astype(F32)
            rk = lax.rsqrt(jnp.sum(kf * kf, axis=1, keepdims=True) + 1e-6)
            keys.append((k, kf, rk))
            colmat = jnp.where(tj == h, rk, colmat)
        rowmat = jnp.transpose(colmat)
        for h in range(0, heads, 2):
            two = slice(h * DH, (h + 2) * DH)
            kd = diagonal(keys[h][0], keys[h + 1][0])
            diags.append(kd)
            kk2 = dot(k_ref[part, two], kd, NT)
            qk2 = dot(q_ref[part, two], kd, NT)
            products.append((kk2[:, :CHUNK], qk2[:, :CHUNK]))
            products.append((kk2[:, CHUNK:], qk2[:, CHUNK:]))
        for h in range(heads):
            k, kf, rk_c = keys[h]
            kk, qk = products[c * heads + h]
            rk_r = rowmat[h : h + 1]
            qf = q_ref[part, h * DH : (h + 1) * DH].astype(F32)
            rq_c = lax.rsqrt(jnp.sum(qf * qf, axis=1, keepdims=True) + 1e-6)
            g_c = cols[:, h : h + 1]
            g_r = rows[h : h + 1]
            b_c = cols[:, heads + h : heads + h + 1]
            b_r = rows[heads + h : heads + h + 1]
            decay = jnp.exp(jnp.where(ti >= tj, g_c - g_r, NEG)) * rk_r
            a = beside(*halves(decay * rq_c * qk))
            low = jnp.where(ti > tj, decay * (b_c * rk_c) * kk, 0.0)
            ts.append(eye - jnp.where((ti >> 1) == (tj >> 1), low, 0.0))
            state.append((kf, rk_c, rk_r, qf, rq_c, g_c, g_r, b_r, a, low))
    count = per * heads
    for shift in range(1, 7):
        pair = (ti >> (shift + 1)) == (tj >> (shift + 1))
        cross = pair & (((ti >> shift) & 1) == 1) & (((tj >> shift) & 1) == 0)
        size = 1 << shift
        tb = [t.astype(BF16) for t in ts]
        lead = [odd_rows(t, size).astype(BF16) for t in ts] if size >= 8 else tb
        lm = [below(*halves(jnp.where(cross, s[-1], 0.0))) for s in state]
        mid = [dot(beside(x, x), y).astype(BF16) for x, y in zip(lead, lm)]
        change = []
        for n in range(0, count, 2):
            both = dot(beside(mid[n], mid[n + 1]), diagonal(tb[n], tb[n + 1]))
            change += [both[:, :CHUNK], both[:, CHUNK:]]
        if size >= 8:
            ts = [less_odd_rows(t, x, size) for t, x in zip(ts, change)]
        else:
            ts = [t - x for t, x in zip(ts, change)]
    ws = []
    for n in range(0, count, 2):
        lead = []
        for s, t in zip(state[n : n + 2], ts[n : n + 2]):
            lead.append((t * (s[7] * jnp.exp(s[6]) * s[2])).astype(BF16))
        both = dot(beside(*lead), diags[n // 2])
        ws += [both[:, :DH], both[:, DH:]]
    starts = []
    for n in range(count):
        c, h = n // heads, n % heads
        kf, rk_c, rk_r, qf, rq_c, g_c, g_r, b_r, a, low = state[n]
        t, w = ts[n], ws[n]
        tail_c = jnp.exp(g_r[:, CHUNK - 1 : CHUNK] - g_c) * rk_c
        tw = beside(t.astype(BF16), w.astype(BF16))
        both = dot(a, below(tw, tw))
        m_ref[c, h] = (both[:, :CHUNK] * b_r).astype(BF16)
        qe = (jnp.exp(g_c) * rq_c) * qf - both[:, CHUNK:]
        kt = jnp.transpose(kf).astype(BF16)
        th, tl = halves(tail_c * t * b_r)
        wh, wl = halves(tail_c * w)
        both = dot(beside(kt, kt), below(beside(th, wh), beside(tl, wl)))
        ke_ref[c, h] = beside(*halves(both[:, :CHUNK]))
        e = -both[:, CHUNK:]
        qeb, eb = qe.astype(BF16), e.astype(BF16)
        qe_ref[c, h] = qeb
        e_ref[c, h] = eb
        starts.append((qe, e, below(qeb, eb), jnp.broadcast_to(jnp.exp(g_r[:, CHUNK - 1 : CHUNK]), (1, DH))))
    for c in range(per):
        for h in range(0, heads, 2):
            ones = starts[c * heads + h : c * heads + h + 2]
            fs = [f_scr[h], f_scr[h + 1]]
            both = dot(beside(ones[0][2], ones[1][2]), diagonal(fs[0].astype(BF16), fs[1].astype(BF16)))
            for n, (qe, e, _, gc) in enumerate(ones):
                part = both[:, n * DH : (n + 1) * DH]
                gp = gp_scr[h + n : h + n + 1]
                qf_ref[c, h + n] = beside(*halves(gp * qe + part[:CHUNK]))
                f_scr[h + n] = gc * fs[n] + gp * e + part[CHUNK:]
                gp_scr[h + n : h + n + 1] = gp * gc
                g_ref[c, h + n : h + n + 1] = gc

    @pl.when(step == pl.num_programs(0) - 1)
    def _():
        for h in range(heads):
            matrix = jnp.transpose(f_scr[h]).astype(BF16)
            gain = pack_gain(gp_scr[h : h + 1])
            for copy in range(w_ref.shape[0] // heads):
                w_ref[h * (w_ref.shape[0] // heads) + copy, :DH] = matrix
                w_ref[h * (w_ref.shape[0] // heads) + copy, DH:] = gain


PER = 4


def prep(log_decay, beta, delta_key, delta_query, copies):
    heads, rows = log_decay.shape
    chunks = rows // CHUNK
    big = jax.ShapeDtypeStruct((chunks, heads, CHUNK, DH), BF16)
    wide = jax.ShapeDtypeStruct((chunks, heads, CHUNK, 2 * DH), BF16)
    big_spec = pl.BlockSpec((PER, heads, CHUNK, DH), lambda c: (c, 0, 0, 0))
    wide_spec = pl.BlockSpec((PER, heads, CHUNK, 2 * DH), lambda c: (c, 0, 0, 0))
    row_spec = pl.BlockSpec((heads, PER * CHUNK), lambda c: (0, c))
    tok_spec = pl.BlockSpec((PER * CHUNK, heads * DH), lambda c: (c, 0))
    return pl.pallas_call(
        functools.partial(prep_kernel, heads, PER),
        grid=(chunks // PER,),
        in_specs=[row_spec, row_spec, tok_spec, tok_spec],
        out_specs=[big_spec, wide_spec, big_spec, wide_spec, big_spec]
        + [
            pl.BlockSpec((PER, heads, DH), lambda c: (c, 0, 0)),
            pl.BlockSpec((heads * copies, WIRE, DH), lambda c: (0, 0, 0)),
        ],
        out_shape=[big, wide, big, wide, big]
        + [
            jax.ShapeDtypeStruct((chunks, heads, DH), F32),
            jax.ShapeDtypeStruct((heads * copies, WIRE, DH), BF16),
        ],
        scratch_shapes=[pltpu.VMEM((heads, DH, DH), F32), pltpu.VMEM((heads, DH), F32)],
        compiler_params=pltpu.CompilerParams(vmem_limit_bytes=VMEM),
        cost_estimate=pl.CostEstimate(flops=1_000_000, bytes_accessed=1_000_000, transcendentals=0),
        name="delta_prep",
    )(log_decay, beta, delta_key, delta_query)


QB = 256
SCALE = 1.0 / math.sqrt(DH) * math.log2(math.e)


def own_kernel(q_ref, k_ref, v_ref, o_ref, vx):
    rows = q_ref.shape[0]
    vx[:, :DH] = v_ref[...]
    vx[:, DH:] = jnp.ones((rows, DH), BF16)
    ri = lax.broadcasted_iota(jnp.int32, (QB, QB), 0)
    rj = lax.broadcasted_iota(jnp.int32, (QB, QB), 1)
    lane = lax.broadcasted_iota(jnp.int32, (QB, DH), 1)
    blocks = [slice(i * QB, (i + 1) * QB) for i in range(rows // QB)]
    scores = []
    for here in blocks:
        s = dot(q_ref[here], k_ref[: here.stop], NT)
        edge = jnp.where(rj <= ri, s[:, here], NEG)
        scores.append(beside(s[:, : here.start], edge) if here.start else edge)
    for here, s in zip(blocks, scores):
        top = jnp.max(s, axis=1, keepdims=True)
        pv = dot(jnp.exp2((s - top) * SCALE).astype(BF16), vx[: here.stop])
        o_ref[here, :DH] = pv[:, :DH]
        o_ref[here, DH:] = jnp.where(lane < DH // 2, pv[:, DH:], top)


def own_part(att_query, att_key, att_value):
    rows, width = att_query.shape
    heads = width // DH
    tok = pl.BlockSpec((rows, DH), lambda h: (0, h))
    return pl.pallas_call(
        own_kernel,
        grid=(heads,),
        in_specs=[tok, tok, tok],
        out_specs=pl.BlockSpec((rows, 2 * DH), lambda h: (0, h)),
        out_shape=jax.ShapeDtypeStruct((rows, 2 * width), F32),
        scratch_shapes=[pltpu.VMEM((rows, 2 * DH), BF16)],
        compiler_params=pltpu.CompilerParams(vmem_limit_bytes=VMEM),
        cost_estimate=pl.CostEstimate(flops=100_000_000_000, bytes_accessed=1_000_000, transcendentals=0),
        name="own_attention",
    )(att_query, att_key, att_value)


def attend_kernel(
    base, first_ref, q_ref, kp_ref, ko_ref, vp_ref, own_ref, m_ref, ke_ref, qe_ref, e_ref, g_ref, *rest
):
    r_ref, b_ref, kx, vx = rest[-4:]
    h = pl.program_id(0) + base
    first = first_ref[0]
    window = kp_ref.shape[0]
    vx[:, :DH] = vp_ref[...]

    @pl.when(first == 0)
    def _():
        kx[...] = kp_ref[...]
        vx[:, DH:] = jnp.ones((window, DH), BF16)

    @pl.when(first != 0)
    def _():
        kx[...] = jnp.broadcast_to(ko_ref[0:1].astype(F32), (window, DH)).astype(BF16)
        vx[:, DH:] = jnp.zeros((window, DH), BF16)

    ri = lax.broadcasted_iota(jnp.int32, (QB, QB), 0)
    rj = lax.broadcasted_iota(jnp.int32, (QB, QB), 1)
    mean = jnp.full((DH, DH), 1.0 / DH, BF16)
    blocks = [slice(i * QB, (i + 1) * QB) for i in range(q_ref.shape[0] // QB)]
    scores = []
    for i, here in enumerate(blocks):
        s = dot(q_ref[here], kx[i * QB :], NT)
        edge = jnp.where(rj > ri, s[:, :QB], NEG)
        scores.append(beside(edge, s[:, QB:]) if s.shape[1] > QB else edge)
    sums = []
    for i, (here, s) in enumerate(zip(blocks, scores)):
        own_top = own_ref[here, 2 * DH - 1 :]
        top = jnp.maximum(jnp.max(s, axis=1, keepdims=True), own_top)
        pv = dot(jnp.exp2((s - top) * SCALE).astype(BF16), vx[i * QB :])
        sums.append((pv, jnp.exp2((own_top - top) * SCALE)))
    outs = []
    for here, (pv, fade) in zip(blocks, sums):
        total = pv[:, DH:] + fade * own_ref[here, DH : DH + 1]
        outs.append(((pv[:, :DH] + fade * own_ref[here, :DH]) / total).astype(BF16).astype(F32))
    squares = [dot(beside(*halves(o * o)), below(mean, mean)) for o in outs]
    values = [halves(o * lax.rsqrt(square + 1e-6)) for o, square in zip(outs, squares)]
    per = QB // CHUNK
    chunks = []
    for c in range(m_ref.shape[0]):
        part = slice((c % per) * CHUNK, (c % per + 1) * CHUNK)
        chunks.append((values[c // per][0][part], values[c // per][1][part]))
    fresh = []
    for c, (vh, vl) in enumerate(chunks):
        ke = ke_ref[c, 0]
        fresh.append(dot(ke, below(vh, vh)) + dot(ke[:, :DH], vl))
    x = jnp.zeros((DH, DH), F32)
    states = []
    for c in range(len(chunks)):
        xh, xl = halves(x)
        states.append(below(xh, xl))
        x = g_ref[c, pl.ds(h, 1)] * x + dot(e_ref[c, 0], xh) + fresh[c]
    for c, (vh, vl) in enumerate(chunks):
        m, qe = m_ref[c, 0], qe_ref[c, 0]
        r_ref[c * CHUNK : (c + 1) * CHUNK] = dot(beside(m, m), below(vh, vl)) + dot(beside(qe, qe), states[c])
    b_ref[0] = jnp.transpose(x).astype(BF16)


def attend(base, first, att_query, kv_prev, k_own, own, m, ke, qe, e, g, *earlier):
    rows, width = att_query.shape
    heads = width // DH
    window, held = kv_prev.shape
    held = held // (2 * DH)
    chunks = rows // CHUNK
    big = pl.BlockSpec((chunks, 1, CHUNK, DH), lambda h: (0, h + base, 0, 0))
    tok = pl.BlockSpec((rows, DH), lambda h: (0, h + base))
    return pl.pallas_call(
        functools.partial(attend_kernel, base),
        grid=(held,),
        in_specs=[
            pl.BlockSpec(memory_space=pltpu.SMEM),
            tok,
            pl.BlockSpec((window, DH), lambda h: (0, h)),
            pl.BlockSpec((16, DH), lambda h: (0, h + base)),
            pl.BlockSpec((window, DH), lambda h: (0, h + held)),
            pl.BlockSpec((rows, 2 * DH), lambda h: (0, h + base)),
            big,
            pl.BlockSpec((chunks, 1, CHUNK, 2 * DH), lambda h: (0, h + base, 0, 0)),
            big,
            big,
            pl.BlockSpec((chunks, heads, DH), lambda h: (0, 0, 0)),
        ]
        + [pl.BlockSpec(memory_space=pl.ANY)] * len(earlier),
        out_specs=[tok, pl.BlockSpec((1, DH, DH), lambda h: (h + base, 0, 0))],
        out_shape=[
            jax.ShapeDtypeStruct((rows, width), F32),
            jax.ShapeDtypeStruct((heads, DH, DH), BF16),
        ],
        input_output_aliases={11 + n: n for n in range(len(earlier))},
        scratch_shapes=[pltpu.VMEM((window, DH), BF16), pltpu.VMEM((window, 2 * DH), BF16)],
        compiler_params=pltpu.CompilerParams(vmem_limit_bytes=MIDDLE),
        cost_estimate=pl.CostEstimate(flops=100_000_000_000, bytes_accessed=1_000_000, transcendentals=0),
        name="window_attention",
    )(first, att_query, kv_prev, k_own, kv_prev, own, m, ke, qe, e, g, *earlier)


def vmem_call(kernel, outs, name, *args):
    vm = pl.BlockSpec(memory_space=pltpu.VMEM)
    return pl.pallas_call(
        kernel,
        in_specs=[vm] * len(args),
        out_specs=[vm] * len(outs),
        out_shape=[jax.ShapeDtypeStruct(*o) for o in outs],
        compiler_params=pltpu.CompilerParams(vmem_limit_bytes=SMALL),
        cost_estimate=pl.CostEstimate(flops=1_000_000, bytes_accessed=1_000_000, transcendentals=0),
        name=name,
    )(*args)


def follow(g, f, d_ref):
    d = d_ref[:DH]
    step = unpack_gain(d_ref[DH:])
    return g * step, step * f + g * d.astype(F32) + dot(f.astype(BF16), d)


def prefix_kernel(d_ref, p_ref, t_ref):
    g = jnp.ones((1, DH), F32)
    f = jnp.zeros((DH, DH), F32)
    count = d_ref.shape[0]
    for z in range(count):
        p_ref[z, :DH] = f.astype(BF16)
        p_ref[z, DH:] = pack_gain(g)
        g, f = follow(g, f, d_ref.at[z])
    t_ref[:DH] = f.astype(BF16)
    t_ref[DH:] = pack_gain(g)


def line_kernel(d_ref, t_ref, b_ref, q_ref, w_ref):
    acc = b_ref[0].astype(F32)
    q_ref[0] = jnp.zeros_like(acc)
    for z in range(1, d_ref.shape[0]):
        q_ref[z] = acc
        g = unpack_gain(d_ref[z, DH:])
        acc = g * acc + b_ref[z].astype(F32) + dot(acc.astype(BF16), d_ref[z, :DH])
    size = acc.shape[0]
    w_ref[: 2 * size] = below(*halves(acc))
    w_ref[2 * size :] = t_ref[...]


def place_kernel(majors, *refs):
    wires = refs[: majors - 1]
    p_ref, q_ref, s_ref = refs[majors - 1 :]
    size = q_ref.shape[1]

    def added(wire):
        return wire[:size].astype(F32) + wire[size : 2 * size].astype(F32)

    base = added(wires[0])
    for k in range(1, majors - 1):
        old = wires[k - 1][2 * size : 2 * size + DH]
        step = unpack_gain(wires[k - 1][2 * size + DH :])
        if k == 1:
            g, f = step, old.astype(F32)
        else:
            f, g = step * f + g * old.astype(F32) + dot(old, f.astype(BF16)), g * step
        value = added(wires[k])
        base = base + g * value + dot(value.astype(BF16), f.astype(BF16))
    high = base.astype(BF16)
    for z in range(p_ref.shape[0]):
        out = unpack_gain(p_ref[z, DH:]) * base + q_ref[z] + dot(high, p_ref[z, :DH])
        s_ref[z] = out.astype(BF16)


def finish_kernel(heads, r_ref, qf_ref, s_ref, gate_ref, gain_ref, o_ref):
    gain = gain_ref[...]
    mean = jnp.full((DH, DH), 1.0 / DH, BF16)
    tiles = [
        (slice(c * CHUNK, (c + 1) * CHUNK), slice(h * DH, (h + 1) * DH), c, h)
        for c in range(qf_ref.shape[0])
        for h in range(heads)
    ]
    reads = [r_ref[rows, cols] + dot(qf_ref[c, h], beside(s_ref[h], s_ref[h]), NT) for rows, cols, c, h in tiles]
    squares = [dot(beside(*halves(r * r)), below(mean, mean)) for r in reads]
    for (rows, cols, c, h), r, square in zip(tiles, reads, squares):
        gate = gate_ref[rows, cols].astype(F32)
        r = r * lax.rsqrt(square + 1e-6) * gain
        o_ref[rows, cols] = (r * (gate / (1.0 + jnp.exp(-gate)))).astype(BF16)


def finish(readout, qf, state, out_gate, gain):
    rows, width = readout.shape
    heads = width // DH
    tok = pl.BlockSpec((PER * CHUNK, width), lambda c: (c, 0))
    return pl.pallas_call(
        functools.partial(finish_kernel, heads),
        grid=(rows // (PER * CHUNK),),
        in_specs=[
            tok,
            pl.BlockSpec((PER, heads, CHUNK, 2 * DH), lambda c: (c, 0, 0, 0)),
            pl.BlockSpec((heads, DH, DH), lambda c: (0, 0, 0)),
            tok,
            pl.BlockSpec((1, DH), lambda c: (0, 0)),
        ],
        out_specs=tok,
        out_shape=jax.ShapeDtypeStruct((rows, width), BF16),
        compiler_params=pltpu.CompilerParams(vmem_limit_bytes=VMEM),
        cost_estimate=pl.CostEstimate(flops=140_000_000, bytes_accessed=6_000_000, transcendentals=600_000),
        name="gated_readout",
    )(readout, qf, state, out_gate, gain)


def body(att_query, att_key, att_value, delta_query, delta_key, out_gate, log_decay, beta, norm_gain):
    heads = log_decay.shape[0]
    count = lax.axis_size("seq")
    minor = 2 * heads
    majors = count // minor
    place = lax.axis_index("seq")
    onward = [(s, s + 1) for s in range(count - 1)]
    copies = minor // heads
    last = heads - 1

    def both(begin, end):
        part = slice(begin * DH, end * DH)
        return beside(att_key[:, part], att_value[:, part])

    kv_first = lax.ppermute(both(0, last), "seq", onward)
    m, ke, qe, qf, e, g, wire = prep(log_decay, beta, delta_key, delta_query, copies)
    wire, kv_last = lax.optimization_barrier((wire, both(last, heads)))
    kv_last = lax.ppermute(kv_last, "seq", onward)
    lines = [[x * minor + z for z in range(minor)] for x in range(majors)]
    d_line = lax.all_to_all(wire, "seq", 0, 0, axis_index_groups=lines)
    own = own_part(att_query, att_key, att_value)
    first = jnp.reshape((place == 0).astype(jnp.int32), (1,))
    coefs = (own, m, ke, qe, e, g)
    early = attend(0, first, att_query, kv_first, att_key, *coefs)
    d_line, early = lax.optimization_barrier((d_line, early))
    p_line, d_total = vmem_call(
        prefix_kernel, [(d_line.shape, BF16), (d_line.shape[1:], BF16)], "decay_prefix", d_line
    )
    early, p_line, d_total = lax.optimization_barrier((early, p_line, d_total))
    readout, b = attend(last, first, att_query, kv_last, att_key, *coefs, *early)
    size = DH // copies
    b_line = lax.all_to_all(b.reshape(minor, size, DH), "seq", 0, 0, axis_index_groups=lines)
    q_line, added = vmem_call(
        line_kernel, [(b_line.shape, F32), ((2 * size + WIRE, DH), BF16)], "line_states", d_line, d_total, b_line
    )

    def from_lines(value, back):
        hops = back * minor
        return lax.ppermute(value, "seq", [(s, s + hops) for s in range(count - hops)])

    wires = [from_lines(added, k) for k in range(1, majors)]
    (s_line,) = vmem_call(
        functools.partial(place_kernel, majors), [(b_line.shape, BF16)], "block_states", *wires, p_line, q_line
    )
    state = lax.all_to_all(s_line, "seq", 0, 0, axis_index_groups=lines).reshape(heads, DH, DH)
    return finish(readout, qf, state, out_gate, norm_gain.reshape(1, DH))


def solution(mesh):
    tokens = P(("doc", "seq"), "head")
    gates = P("head", ("doc", "seq"))
    return jax.shard_map(
        body,
        mesh=mesh,
        in_specs=(tokens,) * 6 + (gates, gates, P()),
        out_specs=tokens,
        check_vma=False,
    )
```

```python
import functools
import math

import jax
import jax.numpy as jnp
from jax import lax
from jax.experimental import pallas as pl
from jax.experimental.pallas import tpu as pltpu
from jax.sharding import PartitionSpec as P

CHUNK = 128
DH = 128
WIRE = 144
VMEM = 60 * 2**20
MIDDLE = 58 * 2**20
SMALL = 8 * 2**20
NEG = -1e30
F32 = jnp.float32
BF16 = jnp.bfloat16
NN = (((1,), (0,)), ((), ()))
NT = (((1,), (1,)), ((), ()))


def dot(a, b, dims=NN):
    return lax.dot_general(a, b, dims, preferred_element_type=F32)


def shift_lanes(row, steps):
    lane = lax.broadcasted_iota(jnp.int32, row.shape, 1)
    return jnp.where(lane >= steps, pltpu.roll(row, steps, axis=1), 0.0)


def halves(value):
    high = value.astype(BF16)
    return high, (value - high.astype(F32)).astype(BF16)


def beside(*parts):
    return jnp.concatenate(parts, axis=1)


def below(*parts):
    return jnp.concatenate(parts, axis=0)


def diagonal(one, two):
    return below(beside(one, jnp.zeros_like(two)), beside(jnp.zeros_like(one), two))


def mean_squares(tiles):
    mean = jnp.full((DH, DH), 1.0 / DH, BF16)
    means = diagonal(mean, mean)
    out = []
    for one, two in zip(tiles[::2], tiles[1::2]):
        both = dot(beside((one * one).astype(BF16), (two * two).astype(BF16)), means)
        out += [both[:, :DH], both[:, DH:]]
    return out


def odd_rows(value, size):
    return below(*[value[i : i + size] for i in range(size, value.shape[0], 2 * size)])


def less_odd_rows(value, change, size):
    parts = []
    for n, i in enumerate(range(0, value.shape[0], 2 * size)):
        parts += [value[i : i + size], value[i + size : i + 2 * size] - change[n * size : (n + 1) * size]]
    return below(*parts)


def split_three(g):
    high = g.astype(BF16)
    rest = g - high.astype(F32)
    mid = rest.astype(BF16)
    low = (rest - mid.astype(F32)).astype(BF16)
    return high, mid, low


def pack_gain(g):
    row = lax.broadcasted_iota(jnp.int32, (WIRE - DH, DH), 0)
    high, mid, low = split_three(g)
    block = jnp.where(
        row == 0,
        high.astype(F32),
        jnp.where(row == 1, mid.astype(F32), jnp.where(row == 2, low.astype(F32), 0.0)),
    )
    return block.astype(BF16)


def unpack_gain(block):
    rows = block.astype(F32)
    return rows[0:1] + rows[1:2] + rows[2:3]


def gate_rows(heads, ld, be):
    rows = below(ld, be)
    cum = rows
    for steps in (1, 2, 4, 8, 16, 32, 64):
        cum = cum + shift_lanes(cum, steps)
    row8 = lax.broadcasted_iota(jnp.int32, (2 * heads, CHUNK), 0)
    return jnp.where(row8 < heads, cum, rows)


def prep_kernel(
    heads, per, ld_ref, be_ref, k_ref, q_ref, m_ref, ke_ref, qe_ref, qf_ref, e_ref, g_ref, w_ref, f_scr, gp_scr
):
    step = pl.program_id(0)

    @pl.when(step == 0)
    def _():
        f_scr[...] = jnp.zeros_like(f_scr)
        gp_scr[...] = jnp.ones_like(gp_scr)

    ti = lax.broadcasted_iota(jnp.int32, (CHUNK, CHUNK), 0)
    tj = lax.broadcasted_iota(jnp.int32, (CHUNK, CHUNK), 1)
    eye = jnp.where(ti == tj, 1.0, 0.0)
    state = []
    ts = []
    products = []
    diags = []
    for c in range(per):
        part = slice(c * CHUNK, (c + 1) * CHUNK)
        rows = gate_rows(heads, ld_ref[:, part], be_ref[:, part])
        cols = jnp.transpose(rows)
        keys = []
        colmat = jnp.zeros((CHUNK, CHUNK), F32)
        for h in range(heads):
            k = k_ref[part, h * DH : (h + 1) * DH]
            kf = k.astype(F32)
            rk = lax.rsqrt(jnp.sum(kf * kf, axis=1, keepdims=True) + 1e-6)
            keys.append((k, kf, rk))
            colmat = jnp.where(tj == h, rk, colmat)
        rowmat = jnp.transpose(colmat)
        for h in range(0, heads, 2):
            two = slice(h * DH, (h + 2) * DH)
            kd = diagonal(keys[h][0], keys[h + 1][0])
            diags.append(kd)
            kk2 = dot(k_ref[part, two], kd, NT)
            qk2 = dot(q_ref[part, two], kd, NT)
            products.append((kk2[:, :CHUNK], qk2[:, :CHUNK]))
            products.append((kk2[:, CHUNK:], qk2[:, CHUNK:]))
        for h in range(heads):
            k, kf, rk_c = keys[h]
            kk, qk = products[c * heads + h]
            rk_r = rowmat[h : h + 1]
            qf = q_ref[part, h * DH : (h + 1) * DH].astype(F32)
            rq_c = lax.rsqrt(jnp.sum(qf * qf, axis=1, keepdims=True) + 1e-6)
            g_c = cols[:, h : h + 1]
            g_r = rows[h : h + 1]
            b_c = cols[:, heads + h : heads + h + 1]
            b_r = rows[heads + h : heads + h + 1]
            decay = jnp.exp(jnp.where(ti >= tj, g_c - g_r, NEG)) * rk_r
            a = beside(*halves(decay * rq_c * qk))
            low = jnp.where(ti > tj, decay * (b_c * rk_c) * kk, 0.0)
            ts.append(eye - jnp.where((ti >> 1) == (tj >> 1), low, 0.0))
            state.append((kf, rk_c, rk_r, qf, rq_c, g_c, g_r, b_r, a, low))
    count = per * heads
    for shift in range(1, 7):
        pair = (ti >> (shift + 1)) == (tj >> (shift + 1))
        cross = pair & (((ti >> shift) & 1) == 1) & (((tj >> shift) & 1) == 0)
        size = 1 << shift
        tb = [t.astype(BF16) for t in ts]
        lead = [odd_rows(t, size).astype(BF16) for t in ts] if size >= 8 else tb
        lm = [below(*halves(jnp.where(cross, s[-1], 0.0))) for s in state]
        mid = [dot(beside(x, x), y).astype(BF16) for x, y in zip(lead, lm)]
        change = []
        for n in range(0, count, 2):
            both = dot(beside(mid[n], mid[n + 1]), diagonal(tb[n], tb[n + 1]))
            change += [both[:, :CHUNK], both[:, CHUNK:]]
        if size >= 8:
            ts = [less_odd_rows(t, x, size) for t, x in zip(ts, change)]
        else:
            ts = [t - x for t, x in zip(ts, change)]
    ws = []
    for n in range(0, count, 2):
        lead = []
        for s, t in zip(state[n : n + 2], ts[n : n + 2]):
            lead.append((t * (s[7] * jnp.exp(s[6]) * s[2])).astype(BF16))
        both = dot(beside(*lead), diags[n // 2])
        ws += [both[:, :DH], both[:, DH:]]
    starts = []
    for n in range(count):
        c, h = n // heads, n % heads
        kf, rk_c, rk_r, qf, rq_c, g_c, g_r, b_r, a, low = state[n]
        t, w = ts[n], ws[n]
        tail_c = jnp.exp(g_r[:, CHUNK - 1 : CHUNK] - g_c) * rk_c
        tw = beside(t.astype(BF16), w.astype(BF16))
        both = dot(a, below(tw, tw))
        m_ref[c, h] = (both[:, :CHUNK] * b_r).astype(BF16)
        qe = (jnp.exp(g_c) * rq_c) * qf - both[:, CHUNK:]
        kt = jnp.transpose(kf).astype(BF16)
        th, tl = halves(tail_c * t * b_r)
        wh, wl = halves(tail_c * w)
        both = dot(beside(kt, kt), below(beside(th, wh), beside(tl, wl)))
        ke_ref[c, h] = beside(*halves(both[:, :CHUNK]))
        e = -both[:, CHUNK:]
        qeb, eb = qe.astype(BF16), e.astype(BF16)
        qe_ref[c, h] = qeb
        e_ref[c, h] = eb
        starts.append((qe, e, below(qeb, eb), jnp.broadcast_to(jnp.exp(g_r[:, CHUNK - 1 : CHUNK]), (1, DH))))
    for c in range(per):
        for h in range(0, heads, 2):
            ones = starts[c * heads + h : c * heads + h + 2]
            fs = [f_scr[h], f_scr[h + 1]]
            both = dot(beside(ones[0][2], ones[1][2]), diagonal(fs[0].astype(BF16), fs[1].astype(BF16)))
            for n, (qe, e, _, gc) in enumerate(ones):
                part = both[:, n * DH : (n + 1) * DH]
                gp = gp_scr[h + n : h + n + 1]
                qf_ref[c, h + n] = beside(*halves(gp * qe + part[:CHUNK]))
                f_scr[h + n] = gc * fs[n] + gp * e + part[CHUNK:]
                gp_scr[h + n : h + n + 1] = gp * gc
                g_ref[c, h + n : h + n + 1] = gc

    @pl.when(step == pl.num_programs(0) - 1)
    def _():
        for h in range(heads):
            matrix = jnp.transpose(f_scr[h]).astype(BF16)
            gain = pack_gain(gp_scr[h : h + 1])
            for copy in range(w_ref.shape[0] // heads):
                w_ref[h * (w_ref.shape[0] // heads) + copy, :DH] = matrix
                w_ref[h * (w_ref.shape[0] // heads) + copy, DH:] = gain


PER = 4


def prep(log_decay, beta, delta_key, delta_query, copies):
    heads, rows = log_decay.shape
    chunks = rows // CHUNK
    big = jax.ShapeDtypeStruct((chunks, heads, CHUNK, DH), BF16)
    wide = jax.ShapeDtypeStruct((chunks, heads, CHUNK, 2 * DH), BF16)
    big_spec = pl.BlockSpec((PER, heads, CHUNK, DH), lambda c: (c, 0, 0, 0))
    wide_spec = pl.BlockSpec((PER, heads, CHUNK, 2 * DH), lambda c: (c, 0, 0, 0))
    row_spec = pl.BlockSpec((heads, PER * CHUNK), lambda c: (0, c))
    tok_spec = pl.BlockSpec((PER * CHUNK, heads * DH), lambda c: (c, 0))
    return pl.pallas_call(
        functools.partial(prep_kernel, heads, PER),
        grid=(chunks // PER,),
        in_specs=[row_spec, row_spec, tok_spec, tok_spec],
        out_specs=[big_spec, wide_spec, big_spec, wide_spec, big_spec]
        + [
            pl.BlockSpec((PER, heads, DH), lambda c: (c, 0, 0)),
            pl.BlockSpec((heads * copies, WIRE, DH), lambda c: (0, 0, 0)),
        ],
        out_shape=[big, wide, big, wide, big]
        + [
            jax.ShapeDtypeStruct((chunks, heads, DH), F32),
            jax.ShapeDtypeStruct((heads * copies, WIRE, DH), BF16),
        ],
        scratch_shapes=[pltpu.VMEM((heads, DH, DH), F32), pltpu.VMEM((heads, DH), F32)],
        compiler_params=pltpu.CompilerParams(vmem_limit_bytes=VMEM),
        cost_estimate=pl.CostEstimate(flops=1_000_000, bytes_accessed=1_000_000, transcendentals=0),
        name="delta_prep",
    )(log_decay, beta, delta_key, delta_query)


QB = 256
SCALE = 1.0 / math.sqrt(DH) * math.log2(math.e)


def own_kernel(q_ref, k_ref, v_ref, o_ref, vx):
    rows = q_ref.shape[0]
    vx[:, :DH] = v_ref[...]
    vx[:, DH:] = jnp.ones((rows, DH), BF16)
    ri = lax.broadcasted_iota(jnp.int32, (QB, QB), 0)
    rj = lax.broadcasted_iota(jnp.int32, (QB, QB), 1)
    lane = lax.broadcasted_iota(jnp.int32, (QB, DH), 1)
    blocks = [slice(i * QB, (i + 1) * QB) for i in range(rows // QB)]
    scores = []
    for here in blocks:
        s = dot(q_ref[here], k_ref[: here.stop], NT)
        edge = jnp.where(rj <= ri, s[:, here], NEG)
        scores.append(beside(s[:, : here.start], edge) if here.start else edge)
    for here, s in zip(blocks, scores):
        top = jnp.max(s, axis=1, keepdims=True)
        pv = dot(jnp.exp2((s - top) * SCALE).astype(BF16), vx[: here.stop])
        o_ref[here, :DH] = pv[:, :DH]
        o_ref[here, DH:] = jnp.where(lane < DH // 2, pv[:, DH:], top)


def own_part(att_query, att_key, att_value):
    rows, width = att_query.shape
    heads = width // DH
    tok = pl.BlockSpec((rows, DH), lambda h: (0, h))
    return pl.pallas_call(
        own_kernel,
        grid=(heads,),
        in_specs=[tok, tok, tok],
        out_specs=pl.BlockSpec((rows, 2 * DH), lambda h: (0, h)),
        out_shape=jax.ShapeDtypeStruct((rows, 2 * width), F32),
        scratch_shapes=[pltpu.VMEM((rows, 2 * DH), BF16)],
        compiler_params=pltpu.CompilerParams(vmem_limit_bytes=VMEM),
        cost_estimate=pl.CostEstimate(flops=100_000_000_000, bytes_accessed=1_000_000, transcendentals=0),
        name="own_attention",
    )(att_query, att_key, att_value)


def attend_kernel(
    base, first_ref, q_ref, kp_ref, ko_ref, vp_ref, own_ref, m_ref, ke_ref, qe_ref, e_ref, g_ref, *rest
):
    r_ref, b_ref, kx, vx = rest[-4:]
    h = pl.program_id(0) + base
    first = first_ref[0]
    window = kp_ref.shape[0]
    vx[:, :DH] = vp_ref[...]

    @pl.when(first == 0)
    def _():
        kx[...] = kp_ref[...]
        vx[:, DH:] = jnp.ones((window, DH), BF16)

    @pl.when(first != 0)
    def _():
        kx[...] = jnp.broadcast_to(ko_ref[0:1].astype(F32), (window, DH)).astype(BF16)
        vx[:, DH:] = jnp.zeros((window, DH), BF16)

    ri = lax.broadcasted_iota(jnp.int32, (QB, QB), 0)
    rj = lax.broadcasted_iota(jnp.int32, (QB, QB), 1)
    blocks = [slice(i * QB, (i + 1) * QB) for i in range(q_ref.shape[0] // QB)]
    scores = []
    for i, here in enumerate(blocks):
        s = dot(q_ref[here], kx[i * QB :], NT)
        edge = jnp.where(rj > ri, s[:, :QB], NEG)
        scores.append(beside(edge, s[:, QB:]) if s.shape[1] > QB else edge)
    sums = []
    for i, (here, s) in enumerate(zip(blocks, scores)):
        own_top = own_ref[here, 2 * DH - 1 :]
        top = jnp.maximum(jnp.max(s, axis=1, keepdims=True), own_top)
        pv = dot(jnp.exp2((s - top) * SCALE).astype(BF16), vx[i * QB :])
        sums.append((pv, jnp.exp2((own_top - top) * SCALE)))
    outs = []
    for here, (pv, fade) in zip(blocks, sums):
        total = pv[:, DH:] + fade * own_ref[here, DH : DH + 1]
        outs.append(((pv[:, :DH] + fade * own_ref[here, :DH]) / total).astype(BF16).astype(F32))
    squares = mean_squares(outs)
    values = [halves(o * lax.rsqrt(square + 1e-6)) for o, square in zip(outs, squares)]
    per = QB // CHUNK
    chunks = []
    for c in range(m_ref.shape[0]):
        part = slice((c % per) * CHUNK, (c % per + 1) * CHUNK)
        chunks.append((values[c // per][0][part], values[c // per][1][part]))
    fresh = []
    for c, (vh, vl) in enumerate(chunks):
        ke = ke_ref[c, 0]
        fresh.append(dot(ke, below(vh, vh)) + dot(ke[:, :DH], vl))
    x = jnp.zeros((DH, DH), F32)
    states = []
    for c in range(len(chunks)):
        xh, xl = halves(x)
        states.append(below(xh, xl))
        x = g_ref[c, pl.ds(h, 1)] * x + dot(e_ref[c, 0], xh) + fresh[c]
    for c, (vh, vl) in enumerate(chunks):
        m, qe = m_ref[c, 0], qe_ref[c, 0]
        r_ref[c * CHUNK : (c + 1) * CHUNK] = dot(beside(m, m), below(vh, vl)) + dot(beside(qe, qe), states[c])
    b_ref[0] = jnp.transpose(x).astype(BF16)


def attend(base, first, att_query, kv_prev, k_own, own, m, ke, qe, e, g, *earlier):
    rows, width = att_query.shape
    heads = width // DH
    window, held = kv_prev.shape
    held = held // (2 * DH)
    chunks = rows // CHUNK
    big = pl.BlockSpec((chunks, 1, CHUNK, DH), lambda h: (0, h + base, 0, 0))
    tok = pl.BlockSpec((rows, DH), lambda h: (0, h + base))
    return pl.pallas_call(
        functools.partial(attend_kernel, base),
        grid=(held,),
        in_specs=[
            pl.BlockSpec(memory_space=pltpu.SMEM),
            tok,
            pl.BlockSpec((window, DH), lambda h: (0, h)),
            pl.BlockSpec((16, DH), lambda h: (0, h + base)),
            pl.BlockSpec((window, DH), lambda h: (0, h + held)),
            pl.BlockSpec((rows, 2 * DH), lambda h: (0, h + base)),
            big,
            pl.BlockSpec((chunks, 1, CHUNK, 2 * DH), lambda h: (0, h + base, 0, 0)),
            big,
            big,
            pl.BlockSpec((chunks, heads, DH), lambda h: (0, 0, 0)),
        ]
        + [pl.BlockSpec(memory_space=pl.ANY)] * len(earlier),
        out_specs=[tok, pl.BlockSpec((1, DH, DH), lambda h: (h + base, 0, 0))],
        out_shape=[
            jax.ShapeDtypeStruct((rows, width), F32),
            jax.ShapeDtypeStruct((heads, DH, DH), BF16),
        ],
        input_output_aliases={11 + n: n for n in range(len(earlier))},
        scratch_shapes=[pltpu.VMEM((window, DH), BF16), pltpu.VMEM((window, 2 * DH), BF16)],
        compiler_params=pltpu.CompilerParams(vmem_limit_bytes=MIDDLE),
        cost_estimate=pl.CostEstimate(flops=100_000_000_000, bytes_accessed=1_000_000, transcendentals=0),
        name="window_attention",
    )(first, att_query, kv_prev, k_own, kv_prev, own, m, ke, qe, e, g, *earlier)


def vmem_call(kernel, outs, name, *args):
    vm = pl.BlockSpec(memory_space=pltpu.VMEM)
    return pl.pallas_call(
        kernel,
        in_specs=[vm] * len(args),
        out_specs=[vm] * len(outs),
        out_shape=[jax.ShapeDtypeStruct(*o) for o in outs],
        compiler_params=pltpu.CompilerParams(vmem_limit_bytes=SMALL),
        cost_estimate=pl.CostEstimate(flops=1_000_000, bytes_accessed=1_000_000, transcendentals=0),
        name=name,
    )(*args)


def follow(g, f, d_ref):
    d = d_ref[:DH]
    step = unpack_gain(d_ref[DH:])
    return g * step, step * f + g * d.astype(F32) + dot(f.astype(BF16), d)


def prefix_kernel(d_ref, p_ref, t_ref):
    g = jnp.ones((1, DH), F32)
    f = jnp.zeros((DH, DH), F32)
    count = d_ref.shape[0]
    for z in range(count):
        p_ref[z, :DH] = f.astype(BF16)
        p_ref[z, DH:] = pack_gain(g)
        g, f = follow(g, f, d_ref.at[z])
    t_ref[:DH] = f.astype(BF16)
    t_ref[DH:] = pack_gain(g)


def line_kernel(d_ref, t_ref, b_ref, q_ref, w_ref):
    acc = b_ref[0].astype(F32)
    q_ref[0] = jnp.zeros_like(acc)
    for z in range(1, d_ref.shape[0]):
        q_ref[z] = acc
        g = unpack_gain(d_ref[z, DH:])
        acc = g * acc + b_ref[z].astype(F32) + dot(acc.astype(BF16), d_ref[z, :DH])
    size = acc.shape[0]
    wire = below(*halves(acc), t_ref[...])
    for x in range(w_ref.shape[0]):
        w_ref[x] = wire


def place_kernel(w_ref, earlier_ref, p_ref, q_ref, s_ref):
    size = q_ref.shape[1]
    base = jnp.zeros((size, DH), F32)
    for x in range(w_ref.shape[0] - 1):
        added = w_ref[x, :size].astype(F32) + w_ref[x, size : 2 * size].astype(F32)
        if x:
            step = unpack_gain(w_ref[x, 2 * size + DH :])
            added = added + step * base + dot(base.astype(BF16), w_ref[x, 2 * size : 2 * size + DH])
        base = jnp.where(earlier_ref[x : x + 1] > 0.0, added, base)
    high = base.astype(BF16)
    for z in range(p_ref.shape[0]):
        out = unpack_gain(p_ref[z, DH:]) * base + q_ref[z] + dot(high, p_ref[z, :DH])
        s_ref[z] = out.astype(BF16)


def finish_kernel(heads, r_ref, qf_ref, s_ref, gate_ref, gain_ref, o_ref):
    gain = gain_ref[...]
    tiles = [
        (slice(c * CHUNK, (c + 1) * CHUNK), slice(h * DH, (h + 1) * DH), c, h)
        for c in range(qf_ref.shape[0])
        for h in range(heads)
    ]
    reads = [r_ref[rows, cols] + dot(qf_ref[c, h], beside(s_ref[h], s_ref[h]), NT) for rows, cols, c, h in tiles]
    squares = mean_squares(reads)
    for (rows, cols, c, h), r, square in zip(tiles, reads, squares):
        gate = gate_ref[rows, cols].astype(F32)
        r = r * lax.rsqrt(square + 1e-6) * gain
        o_ref[rows, cols] = (r * (gate / (1.0 + jnp.exp(-gate)))).astype(BF16)


def finish(readout, qf, state, out_gate, gain):
    rows, width = readout.shape
    heads = width // DH
    tok = pl.BlockSpec((PER * CHUNK, width), lambda c: (c, 0))
    return pl.pallas_call(
        functools.partial(finish_kernel, heads),
        grid=(rows // (PER * CHUNK),),
        in_specs=[
            tok,
            pl.BlockSpec((PER, heads, CHUNK, 2 * DH), lambda c: (c, 0, 0, 0)),
            pl.BlockSpec((heads, DH, DH), lambda c: (0, 0, 0)),
            tok,
            pl.BlockSpec((1, DH), lambda c: (0, 0)),
        ],
        out_specs=tok,
        out_shape=jax.ShapeDtypeStruct((rows, width), BF16),
        compiler_params=pltpu.CompilerParams(vmem_limit_bytes=VMEM),
        cost_estimate=pl.CostEstimate(flops=140_000_000, bytes_accessed=6_000_000, transcendentals=600_000),
        name="gated_readout",
    )(readout, qf, state, out_gate, gain)


def body(att_query, att_key, att_value, delta_query, delta_key, out_gate, log_decay, beta, norm_gain):
    heads = log_decay.shape[0]
    count = lax.axis_size("seq")
    minor = 2 * heads
    majors = count // minor
    place = lax.axis_index("seq")
    onward = [(s, s + 1) for s in range(count - 1)]
    copies = minor // heads
    last = heads - 1


    def both(begin, end):
        part = slice(begin * DH, end * DH)
        return beside(att_key[:, part], att_value[:, part])

    kv_first = lax.ppermute(both(0, last), "seq", onward)
    m, ke, qe, qf, e, g, wire = prep(log_decay, beta, delta_key, delta_query, copies)
    earlier = (jnp.arange(majors) < place // minor).astype(F32)
    earlier = jnp.broadcast_to(earlier[:, None], (majors, DH))
    wire, kv_last, earlier = lax.optimization_barrier((wire, both(last, heads), earlier))
    kv_last = lax.ppermute(kv_last, "seq", onward)
    lines = [[x * minor + z for z in range(minor)] for x in range(majors)]
    d_line = lax.all_to_all(wire, "seq", 0, 0, axis_index_groups=lines)
    own = own_part(att_query, att_key, att_value)
    first = jnp.reshape((place == 0).astype(jnp.int32), (1,))
    coefs = (own, m, ke, qe, e, g)
    early = attend(0, first, att_query, kv_first, att_key, *coefs)
    d_line, early = lax.optimization_barrier((d_line, early))
    p_line, d_total = vmem_call(
        prefix_kernel, [(d_line.shape, BF16), (d_line.shape[1:], BF16)], "decay_prefix", d_line
    )
    early, p_line, d_total = lax.optimization_barrier((early, p_line, d_total))
    readout, b = attend(last, first, att_query, kv_last, att_key, *coefs, *early)
    size = DH // copies
    b_line = lax.all_to_all(b.reshape(minor, size, DH), "seq", 0, 0, axis_index_groups=lines)
    q_line, added = vmem_call(
        line_kernel, [(b_line.shape, F32), ((majors, 2 * size + WIRE, DH), BF16)], "line_states", d_line, d_total, b_line
    )

    columns = [[x * minor + z for x in range(majors)] for z in range(minor)]
    wires = lax.all_to_all(added, "seq", 0, 0, axis_index_groups=columns)
    (s_line,) = vmem_call(place_kernel, [(b_line.shape, BF16)], "block_states", wires, earlier, p_line, q_line)
    state = lax.all_to_all(s_line, "seq", 0, 0, axis_index_groups=lines).reshape(heads, DH, DH)
    return finish(readout, qf, state, out_gate, norm_gain.reshape(1, DH))


def solution(mesh):
    tokens = P(("doc", "seq"), "head")
    gates = P("head", ("doc", "seq"))
    return jax.shard_map(
        body,
        mesh=mesh,
        in_specs=(tokens,) * 6 + (gates, gates, P()),
        out_specs=tokens,
        check_vma=False,
    )
```

```python
import functools
import math

import jax
import jax.numpy as jnp
from jax import lax
from jax.experimental import pallas as pl
from jax.experimental.pallas import tpu as pltpu
from jax.sharding import PartitionSpec as P

CHUNK = 128
DH = 128
WIRE = 144
VMEM = 60 * 2**20
MIDDLE = 58 * 2**20
SMALL = 8 * 2**20
NEG = -1e30
F32 = jnp.float32
BF16 = jnp.bfloat16
NN = (((1,), (0,)), ((), ()))
NT = (((1,), (1,)), ((), ()))


def dot(a, b, dims=NN):
    return lax.dot_general(a, b, dims, preferred_element_type=F32)


def shift_lanes(row, steps):
    lane = lax.broadcasted_iota(jnp.int32, row.shape, 1)
    return jnp.where(lane >= steps, pltpu.roll(row, steps, axis=1), 0.0)


def halves(value):
    high = value.astype(BF16)
    return high, (value - high.astype(F32)).astype(BF16)


def beside(*parts):
    return jnp.concatenate(parts, axis=1)


def below(*parts):
    return jnp.concatenate(parts, axis=0)


def diagonal(one, two):
    return below(beside(one, jnp.zeros_like(two)), beside(jnp.zeros_like(one), two))


def mean_squares(tiles):
    mean = jnp.full((DH, DH), 1.0 / DH, BF16)
    means = diagonal(mean, mean)
    out = []
    for one, two in zip(tiles[::2], tiles[1::2]):
        both = dot(beside((one * one).astype(BF16), (two * two).astype(BF16)), means)
        out += [both[:, :DH], both[:, DH:]]
    return out


def odd_rows(value, size):
    return below(*[value[i : i + size] for i in range(size, value.shape[0], 2 * size)])


def less_odd_rows(value, change, size):
    parts = []
    for n, i in enumerate(range(0, value.shape[0], 2 * size)):
        parts += [value[i : i + size], value[i + size : i + 2 * size] - change[n * size : (n + 1) * size]]
    return below(*parts)


def split_three(g):
    high = g.astype(BF16)
    rest = g - high.astype(F32)
    mid = rest.astype(BF16)
    low = (rest - mid.astype(F32)).astype(BF16)
    return high, mid, low


def pack_gain(g):
    row = lax.broadcasted_iota(jnp.int32, (WIRE - DH, DH), 0)
    high, mid, low = split_three(g)
    block = jnp.where(
        row == 0,
        high.astype(F32),
        jnp.where(row == 1, mid.astype(F32), jnp.where(row == 2, low.astype(F32), 0.0)),
    )
    return block.astype(BF16)


def unpack_gain(block):
    rows = block.astype(F32)
    return rows[0:1] + rows[1:2] + rows[2:3]


def gate_rows(heads, ld, be):
    rows = below(ld, be)
    cum = rows
    for steps in (1, 2, 4, 8, 16, 32, 64):
        cum = cum + shift_lanes(cum, steps)
    row8 = lax.broadcasted_iota(jnp.int32, (2 * heads, CHUNK), 0)
    return jnp.where(row8 < heads, cum, rows)


def prep_kernel(
    heads, per, ld_ref, be_ref, k_ref, q_ref, m_ref, ke_ref, qe_ref, qf_ref, e_ref, g_ref, w_ref, f_scr, gp_scr
):
    step = pl.program_id(0)

    @pl.when(step == 0)
    def _():
        f_scr[...] = jnp.zeros_like(f_scr)
        gp_scr[...] = jnp.ones_like(gp_scr)

    ti = lax.broadcasted_iota(jnp.int32, (CHUNK, CHUNK), 0)
    tj = lax.broadcasted_iota(jnp.int32, (CHUNK, CHUNK), 1)
    eye = jnp.where(ti == tj, 1.0, 0.0)
    state = []
    ts = []
    products = []
    diags = []
    for c in range(per):
        part = slice(c * CHUNK, (c + 1) * CHUNK)
        rows = gate_rows(heads, ld_ref[:, part], be_ref[:, part])
        cols = jnp.transpose(rows)
        keys = []
        colmat = jnp.zeros((CHUNK, CHUNK), F32)
        for h in range(heads):
            k = k_ref[part, h * DH : (h + 1) * DH]
            kf = k.astype(F32)
            rk = lax.rsqrt(jnp.sum(kf * kf, axis=1, keepdims=True) + 1e-6)
            keys.append((k, kf, rk))
            colmat = jnp.where(tj == h, rk, colmat)
        rowmat = jnp.transpose(colmat)
        for h in range(0, heads, 2):
            two = slice(h * DH, (h + 2) * DH)
            kd = diagonal(keys[h][0], keys[h + 1][0])
            diags.append(kd)
            kk2 = dot(k_ref[part, two], kd, NT)
            qk2 = dot(q_ref[part, two], kd, NT)
            products.append((kk2[:, :CHUNK], qk2[:, :CHUNK]))
            products.append((kk2[:, CHUNK:], qk2[:, CHUNK:]))
        for h in range(heads):
            k, kf, rk_c = keys[h]
            kk, qk = products[c * heads + h]
            rk_r = rowmat[h : h + 1]
            qf = q_ref[part, h * DH : (h + 1) * DH].astype(F32)
            rq_c = lax.rsqrt(jnp.sum(qf * qf, axis=1, keepdims=True) + 1e-6)
            g_c = cols[:, h : h + 1]
            g_r = rows[h : h + 1]
            b_c = cols[:, heads + h : heads + h + 1]
            b_r = rows[heads + h : heads + h + 1]
            decay = jnp.exp(jnp.where(ti >= tj, g_c - g_r, NEG)) * rk_r
            a = beside(*halves(decay * rq_c * qk))
            low = jnp.where(ti > tj, decay * (b_c * rk_c) * kk, 0.0)
            ts.append(eye - jnp.where((ti >> 1) == (tj >> 1), low, 0.0))
            state.append((kf, rk_c, rk_r, qf, rq_c, g_c, g_r, b_r, a, low))
    count = per * heads
    for shift in range(1, 7):
        pair = (ti >> (shift + 1)) == (tj >> (shift + 1))
        cross = pair & (((ti >> shift) & 1) == 1) & (((tj >> shift) & 1) == 0)
        size = 1 << shift
        tb = [t.astype(BF16) for t in ts]
        lead = [odd_rows(t, size).astype(BF16) for t in ts] if size >= 8 else tb
        lm = [below(*halves(jnp.where(cross, s[-1], 0.0))) for s in state]
        mid = [dot(beside(x, x), y).astype(BF16) for x, y in zip(lead, lm)]
        change = []
        for n in range(0, count, 2):
            both = dot(beside(mid[n], mid[n + 1]), diagonal(tb[n], tb[n + 1]))
            change += [both[:, :CHUNK], both[:, CHUNK:]]
        if size >= 8:
            ts = [less_odd_rows(t, x, size) for t, x in zip(ts, change)]
        else:
            ts = [t - x for t, x in zip(ts, change)]
    ws = []
    for n in range(0, count, 2):
        lead = []
        for s, t in zip(state[n : n + 2], ts[n : n + 2]):
            lead.append((t * (s[7] * jnp.exp(s[6]) * s[2])).astype(BF16))
        both = dot(beside(*lead), diags[n // 2])
        ws += [both[:, :DH], both[:, DH:]]
    starts = []
    for n in range(count):
        c, h = n // heads, n % heads
        kf, rk_c, rk_r, qf, rq_c, g_c, g_r, b_r, a, low = state[n]
        t, w = ts[n], ws[n]
        tail_c = jnp.exp(g_r[:, CHUNK - 1 : CHUNK] - g_c) * rk_c
        tw = beside(t.astype(BF16), w.astype(BF16))
        both = dot(a, below(tw, tw))
        m_ref[c, h] = (both[:, :CHUNK] * b_r).astype(BF16)
        qe = (jnp.exp(g_c) * rq_c) * qf - both[:, CHUNK:]
        kt = jnp.transpose(kf).astype(BF16)
        th, tl = halves(tail_c * t * b_r)
        wh, wl = halves(tail_c * w)
        both = dot(beside(kt, kt), below(beside(th, wh), beside(tl, wl)))
        ke_ref[c, h] = beside(*halves(both[:, :CHUNK]))
        e = -both[:, CHUNK:]
        qeb, eb = qe.astype(BF16), e.astype(BF16)
        qe_ref[c, h] = qeb
        e_ref[c, h] = eb
        starts.append((qe, e, below(qeb, eb), jnp.broadcast_to(jnp.exp(g_r[:, CHUNK - 1 : CHUNK]), (1, DH))))
    for c in range(per):
        for h in range(0, heads, 2):
            ones = starts[c * heads + h : c * heads + h + 2]
            fs = [f_scr[h], f_scr[h + 1]]
            both = dot(beside(ones[0][2], ones[1][2]), diagonal(fs[0].astype(BF16), fs[1].astype(BF16)))
            for n, (qe, e, _, gc) in enumerate(ones):
                part = both[:, n * DH : (n + 1) * DH]
                gp = gp_scr[h + n : h + n + 1]
                qf_ref[c, h + n] = beside(*halves(gp * qe + part[:CHUNK]))
                f_scr[h + n] = gc * fs[n] + gp * e + part[CHUNK:]
                gp_scr[h + n : h + n + 1] = gp * gc
                g_ref[c, h + n : h + n + 1] = gc

    @pl.when(step == pl.num_programs(0) - 1)
    def _():
        for h in range(heads):
            matrix = jnp.transpose(f_scr[h]).astype(BF16)
            gain = pack_gain(gp_scr[h : h + 1])
            for copy in range(w_ref.shape[0] // heads):
                w_ref[h * (w_ref.shape[0] // heads) + copy, :DH] = matrix
                w_ref[h * (w_ref.shape[0] // heads) + copy, DH:] = gain


PER = 4


def prep(log_decay, beta, delta_key, delta_query, copies):
    heads, rows = log_decay.shape
    chunks = rows // CHUNK
    big = jax.ShapeDtypeStruct((chunks, heads, CHUNK, DH), BF16)
    wide = jax.ShapeDtypeStruct((chunks, heads, CHUNK, 2 * DH), BF16)
    big_spec = pl.BlockSpec((PER, heads, CHUNK, DH), lambda c: (c, 0, 0, 0))
    wide_spec = pl.BlockSpec((PER, heads, CHUNK, 2 * DH), lambda c: (c, 0, 0, 0))
    row_spec = pl.BlockSpec((heads, PER * CHUNK), lambda c: (0, c))
    tok_spec = pl.BlockSpec((PER * CHUNK, heads * DH), lambda c: (c, 0))
    return pl.pallas_call(
        functools.partial(prep_kernel, heads, PER),
        grid=(chunks // PER,),
        in_specs=[row_spec, row_spec, tok_spec, tok_spec],
        out_specs=[big_spec, wide_spec, big_spec, wide_spec, big_spec]
        + [
            pl.BlockSpec((PER, heads, DH), lambda c: (c, 0, 0)),
            pl.BlockSpec((heads * copies, WIRE, DH), lambda c: (0, 0, 0)),
        ],
        out_shape=[big, wide, big, wide, big]
        + [
            jax.ShapeDtypeStruct((chunks, heads, DH), F32),
            jax.ShapeDtypeStruct((heads * copies, WIRE, DH), BF16),
        ],
        scratch_shapes=[pltpu.VMEM((heads, DH, DH), F32), pltpu.VMEM((heads, DH), F32)],
        compiler_params=pltpu.CompilerParams(vmem_limit_bytes=VMEM),
        cost_estimate=pl.CostEstimate(flops=1_000_000, bytes_accessed=1_000_000, transcendentals=0),
        name="delta_prep",
    )(log_decay, beta, delta_key, delta_query)


QB = 256
SCALE = 1.0 / math.sqrt(DH) * math.log2(math.e)


def own_kernel(q_ref, k_ref, v_ref, o_ref, vx):
    rows = q_ref.shape[0]
    vx[:, :DH] = v_ref[...]
    vx[:, DH:] = jnp.ones((rows, DH), BF16)
    ri = lax.broadcasted_iota(jnp.int32, (QB, QB), 0)
    rj = lax.broadcasted_iota(jnp.int32, (QB, QB), 1)
    lane = lax.broadcasted_iota(jnp.int32, (QB, DH), 1)
    blocks = [slice(i * QB, (i + 1) * QB) for i in range(rows // QB)]
    scores = []
    for here in blocks:
        s = dot(q_ref[here], k_ref[: here.stop], NT)
        edge = jnp.where(rj <= ri, s[:, here], NEG)
        scores.append(beside(s[:, : here.start], edge) if here.start else edge)
    for here, s in zip(blocks, scores):
        top = jnp.max(s, axis=1, keepdims=True)
        pv = dot(jnp.exp2((s - top) * SCALE).astype(BF16), vx[: here.stop])
        o_ref[here, :DH] = pv[:, :DH]
        o_ref[here, DH:] = jnp.where(lane < DH // 2, pv[:, DH:], top)


def own_part(att_query, att_key, att_value):
    rows, width = att_query.shape
    heads = width // DH
    tok = pl.BlockSpec((rows, DH), lambda h: (0, h))
    return pl.pallas_call(
        own_kernel,
        grid=(heads,),
        in_specs=[tok, tok, tok],
        out_specs=pl.BlockSpec((rows, 2 * DH), lambda h: (0, h)),
        out_shape=jax.ShapeDtypeStruct((rows, 2 * width), F32),
        scratch_shapes=[pltpu.VMEM((rows, 2 * DH), BF16)],
        compiler_params=pltpu.CompilerParams(vmem_limit_bytes=VMEM),
        cost_estimate=pl.CostEstimate(flops=100_000_000_000, bytes_accessed=1_000_000, transcendentals=0),
        name="own_attention",
    )(att_query, att_key, att_value)


def attend_kernel(
    base, first_ref, q_ref, kp_ref, ko_ref, vp_ref, own_ref, m_ref, ke_ref, qe_ref, e_ref, g_ref, *rest
):
    r_ref, b_ref, kx, vx = rest[-4:]
    h = pl.program_id(0) + base
    first = first_ref[0]
    window = kp_ref.shape[0]
    vx[:, :DH] = vp_ref[...]

    @pl.when(first == 0)
    def _():
        kx[...] = kp_ref[...]
        vx[:, DH:] = jnp.ones((window, DH), BF16)

    @pl.when(first != 0)
    def _():
        kx[...] = jnp.broadcast_to(ko_ref[0:1].astype(F32), (window, DH)).astype(BF16)
        vx[:, DH:] = jnp.zeros((window, DH), BF16)

    ri = lax.broadcasted_iota(jnp.int32, (QB, QB), 0)
    rj = lax.broadcasted_iota(jnp.int32, (QB, QB), 1)
    blocks = [slice(i * QB, (i + 1) * QB) for i in range(q_ref.shape[0] // QB)]
    scores = []
    for i, here in enumerate(blocks):
        s = dot(q_ref[here], kx[i * QB :], NT)
        edge = jnp.where(rj > ri, s[:, :QB], NEG)
        scores.append(beside(edge, s[:, QB:]) if s.shape[1] > QB else edge)
    sums = []
    for i, (here, s) in enumerate(zip(blocks, scores)):
        own_top = own_ref[here, 2 * DH - 1 :]
        top = jnp.maximum(jnp.max(s, axis=1, keepdims=True), own_top)
        pv = dot(jnp.exp2((s - top) * SCALE).astype(BF16), vx[i * QB :])
        sums.append((pv, jnp.exp2((own_top - top) * SCALE)))
    outs = []
    for here, (pv, fade) in zip(blocks, sums):
        total = pv[:, DH:] + fade * own_ref[here, DH : DH + 1]
        outs.append(((pv[:, :DH] + fade * own_ref[here, :DH]) / total).astype(BF16).astype(F32))
    squares = mean_squares(outs)
    values = [halves(o * lax.rsqrt(square + 1e-6)) for o, square in zip(outs, squares)]
    per = QB // CHUNK
    chunks = []
    for c in range(m_ref.shape[0]):
        part = slice((c % per) * CHUNK, (c % per + 1) * CHUNK)
        chunks.append((values[c // per][0][part], values[c // per][1][part]))
    fresh = []
    for c, (vh, vl) in enumerate(chunks):
        ke = ke_ref[c, 0]
        fresh.append(dot(ke, below(vh, vh)) + dot(ke[:, :DH], vl))
    x = jnp.zeros((DH, DH), F32)
    states = []
    for c in range(len(chunks)):
        xh, xl = halves(x)
        states.append(below(xh, xl))
        x = g_ref[c, pl.ds(h, 1)] * x + dot(e_ref[c, 0], xh) + fresh[c]
    for c, (vh, vl) in enumerate(chunks):
        m, qe = m_ref[c, 0], qe_ref[c, 0]
        r_ref[c * CHUNK : (c + 1) * CHUNK] = dot(beside(m, m), below(vh, vl)) + dot(beside(qe, qe), states[c])
    b_ref[0] = jnp.transpose(x).astype(BF16)


def attend(base, first, att_query, kv_prev, k_own, own, m, ke, qe, e, g, *earlier):
    rows, width = att_query.shape
    heads = width // DH
    window, held = kv_prev.shape
    held = held // (2 * DH)
    chunks = rows // CHUNK
    big = pl.BlockSpec((chunks, 1, CHUNK, DH), lambda h: (0, h + base, 0, 0))
    tok = pl.BlockSpec((rows, DH), lambda h: (0, h + base))
    return pl.pallas_call(
        functools.partial(attend_kernel, base),
        grid=(held,),
        in_specs=[
            pl.BlockSpec(memory_space=pltpu.SMEM),
            tok,
            pl.BlockSpec((window, DH), lambda h: (0, h)),
            pl.BlockSpec((16, DH), lambda h: (0, h + base)),
            pl.BlockSpec((window, DH), lambda h: (0, h + held)),
            pl.BlockSpec((rows, 2 * DH), lambda h: (0, h + base)),
            big,
            pl.BlockSpec((chunks, 1, CHUNK, 2 * DH), lambda h: (0, h + base, 0, 0)),
            big,
            big,
            pl.BlockSpec((chunks, heads, DH), lambda h: (0, 0, 0)),
        ]
        + [pl.BlockSpec(memory_space=pl.ANY)] * len(earlier),
        out_specs=[tok, pl.BlockSpec((1, DH, DH), lambda h: (h + base, 0, 0))],
        out_shape=[
            jax.ShapeDtypeStruct((rows, width), F32),
            jax.ShapeDtypeStruct((heads, DH, DH), BF16),
        ],
        input_output_aliases={11 + n: n for n in range(len(earlier))},
        scratch_shapes=[pltpu.VMEM((window, DH), BF16), pltpu.VMEM((window, 2 * DH), BF16)],
        compiler_params=pltpu.CompilerParams(vmem_limit_bytes=MIDDLE),
        cost_estimate=pl.CostEstimate(flops=1_000_000 if earlier else 100_000_000_000, bytes_accessed=1_000_000, transcendentals=0),
        name="window_attention",
    )(first, att_query, kv_prev, k_own, kv_prev, own, m, ke, qe, e, g, *earlier)


def vmem_call(kernel, outs, name, *args):
    vm = pl.BlockSpec(memory_space=pltpu.VMEM)
    return pl.pallas_call(
        kernel,
        in_specs=[vm] * len(args),
        out_specs=[vm] * len(outs),
        out_shape=[jax.ShapeDtypeStruct(*o) for o in outs],
        compiler_params=pltpu.CompilerParams(vmem_limit_bytes=SMALL),
        cost_estimate=pl.CostEstimate(flops=1_000_000, bytes_accessed=1_000_000, transcendentals=0),
        name=name,
    )(*args)


def follow(g, f, d_ref):
    d = d_ref[:DH]
    step = unpack_gain(d_ref[DH:])
    return g * step, step * f + g * d.astype(F32) + dot(f.astype(BF16), d)


def prefix_kernel(d_ref, p_ref, t_ref):
    g = jnp.ones((1, DH), F32)
    f = jnp.zeros((DH, DH), F32)
    count = d_ref.shape[0]
    for z in range(count):
        p_ref[z, :DH] = f.astype(BF16)
        p_ref[z, DH:] = pack_gain(g)
        g, f = follow(g, f, d_ref.at[z])
    t_ref[:DH] = f.astype(BF16)
    t_ref[DH:] = pack_gain(g)


def line_kernel(d_ref, t_ref, b_ref, q_ref, w_ref):
    acc = b_ref[0].astype(F32)
    q_ref[0] = jnp.zeros_like(acc)
    for z in range(1, d_ref.shape[0]):
        q_ref[z] = acc
        g = unpack_gain(d_ref[z, DH:])
        acc = g * acc + b_ref[z].astype(F32) + dot(acc.astype(BF16), d_ref[z, :DH])
    size = acc.shape[0]
    wire = below(*halves(acc), t_ref[...])
    for x in range(w_ref.shape[0]):
        w_ref[x] = wire


def place_kernel(w_ref, earlier_ref, p_ref, q_ref, s_ref):
    size = q_ref.shape[1]
    base = jnp.zeros((size, DH), F32)
    for x in range(w_ref.shape[0] - 1):
        added = w_ref[x, :size].astype(F32) + w_ref[x, size : 2 * size].astype(F32)
        if x:
            step = unpack_gain(w_ref[x, 2 * size + DH :])
            added = added + step * base + dot(base.astype(BF16), w_ref[x, 2 * size : 2 * size + DH])
        base = jnp.where(earlier_ref[x : x + 1] > 0.0, added, base)
    high = base.astype(BF16)
    for z in range(p_ref.shape[0]):
        out = unpack_gain(p_ref[z, DH:]) * base + q_ref[z] + dot(high, p_ref[z, :DH])
        s_ref[z] = out.astype(BF16)


def finish_kernel(heads, r_ref, qf_ref, s_ref, gate_ref, gain_ref, o_ref):
    gain = gain_ref[...]
    tiles = [
        (slice(c * CHUNK, (c + 1) * CHUNK), slice(h * DH, (h + 1) * DH), c, h)
        for c in range(qf_ref.shape[0])
        for h in range(heads)
    ]
    reads = [r_ref[rows, cols] + dot(qf_ref[c, h], beside(s_ref[h], s_ref[h]), NT) for rows, cols, c, h in tiles]
    squares = mean_squares(reads)
    for (rows, cols, c, h), r, square in zip(tiles, reads, squares):
        gate = gate_ref[rows, cols].astype(F32)
        r = r * lax.rsqrt(square + 1e-6) * gain
        o_ref[rows, cols] = (r * (gate / (1.0 + jnp.exp(-gate)))).astype(BF16)


def finish(readout, qf, state, out_gate, gain):
    rows, width = readout.shape
    heads = width // DH
    tok = pl.BlockSpec((PER * CHUNK, width), lambda c: (c, 0))
    return pl.pallas_call(
        functools.partial(finish_kernel, heads),
        grid=(rows // (PER * CHUNK),),
        in_specs=[
            tok,
            pl.BlockSpec((PER, heads, CHUNK, 2 * DH), lambda c: (c, 0, 0, 0)),
            pl.BlockSpec((heads, DH, DH), lambda c: (0, 0, 0)),
            tok,
            pl.BlockSpec((1, DH), lambda c: (0, 0)),
        ],
        out_specs=tok,
        out_shape=jax.ShapeDtypeStruct((rows, width), BF16),
        compiler_params=pltpu.CompilerParams(vmem_limit_bytes=VMEM),
        cost_estimate=pl.CostEstimate(flops=140_000_000, bytes_accessed=6_000_000, transcendentals=600_000),
        name="gated_readout",
    )(readout, qf, state, out_gate, gain)


def body(att_query, att_key, att_value, delta_query, delta_key, out_gate, log_decay, beta, norm_gain):
    heads = log_decay.shape[0]
    count = lax.axis_size("seq")
    minor = 2 * heads
    majors = count // minor
    place = lax.axis_index("seq")
    onward = [(s, s + 1) for s in range(count - 1)]
    copies = minor // heads
    last = heads - 1


    def both(begin, end):
        part = slice(begin * DH, end * DH)
        return beside(att_key[:, part], att_value[:, part])

    kv_first = lax.ppermute(both(0, last), "seq", onward)
    own = own_part(att_query, att_key, att_value)
    earlier = (jnp.arange(majors) < place // minor).astype(F32)
    earlier = jnp.broadcast_to(earlier[:, None], (majors, DH))
    own, kv_last, delta_key, earlier = lax.optimization_barrier((own, both(last, heads), delta_key, earlier))
    kv_last = lax.ppermute(kv_last, "seq", onward)
    m, ke, qe, qf, e, g, wire = prep(log_decay, beta, delta_key, delta_query, copies)
    lines = [[x * minor + z for z in range(minor)] for x in range(majors)]
    d_line = lax.all_to_all(wire, "seq", 0, 0, axis_index_groups=lines)
    first = jnp.reshape((place == 0).astype(jnp.int32), (1,))
    coefs = (own, m, ke, qe, e, g)
    early = attend(0, first, att_query, kv_first, att_key, *coefs)
    readout, b = attend(last, first, att_query, kv_last, att_key, *coefs, *early)
    d_line, b = lax.optimization_barrier((d_line, b))
    p_line, d_total = vmem_call(
        prefix_kernel, [(d_line.shape, BF16), (d_line.shape[1:], BF16)], "decay_prefix", d_line
    )
    b, p_line, d_total = lax.optimization_barrier((b, p_line, d_total))
    size = DH // copies
    b_line = lax.all_to_all(b.reshape(minor, size, DH), "seq", 0, 0, axis_index_groups=lines)
    q_line, added = vmem_call(
        line_kernel, [(b_line.shape, F32), ((majors, 2 * size + WIRE, DH), BF16)], "line_states", d_line, d_total, b_line
    )

    columns = [[x * minor + z for x in range(majors)] for z in range(minor)]
    wires = lax.all_to_all(added, "seq", 0, 0, axis_index_groups=columns)
    (s_line,) = vmem_call(place_kernel, [(b_line.shape, BF16)], "block_states", wires, earlier, p_line, q_line)
    state = lax.all_to_all(s_line, "seq", 0, 0, axis_index_groups=lines).reshape(heads, DH, DH)
    return finish(readout, qf, state, out_gate, norm_gain.reshape(1, DH))


def solution(mesh):
    tokens = P(("doc", "seq"), "head")
    gates = P("head", ("doc", "seq"))
    return jax.shard_map(
        body,
        mesh=mesh,
        in_specs=(tokens,) * 6 + (gates, gates, P()),
        out_specs=tokens,
        check_vma=False,
    )
```

```python
import functools
import math

import jax
import jax.numpy as jnp
from jax import lax
from jax.experimental import pallas as pl
from jax.experimental.pallas import tpu as pltpu
from jax.sharding import PartitionSpec as P

CHUNK = 128
DH = 128
WIRE = 144
VMEM = 60 * 2**20
MIDDLE = 58 * 2**20
SMALL = 8 * 2**20
LATER = 50 * 2**20
NEG = -1e30
F32 = jnp.float32
BF16 = jnp.bfloat16
NN = (((1,), (0,)), ((), ()))
NT = (((1,), (1,)), ((), ()))


def dot(a, b, dims=NN):
    return lax.dot_general(a, b, dims, preferred_element_type=F32)


def shift_lanes(row, steps):
    lane = lax.broadcasted_iota(jnp.int32, row.shape, 1)
    return jnp.where(lane >= steps, pltpu.roll(row, steps, axis=1), 0.0)


def halves(value):
    high = value.astype(BF16)
    return high, (value - high.astype(F32)).astype(BF16)


def beside(*parts):
    return jnp.concatenate(parts, axis=1)


def below(*parts):
    return jnp.concatenate(parts, axis=0)


def diagonal(one, two):
    return below(beside(one, jnp.zeros_like(two)), beside(jnp.zeros_like(one), two))


def mean_squares(tiles):
    mean = jnp.full((DH, DH), 1.0 / DH, BF16)
    means = diagonal(mean, mean)
    out = []
    for one, two in zip(tiles[::2], tiles[1::2]):
        both = dot(beside((one * one).astype(BF16), (two * two).astype(BF16)), means)
        out += [both[:, :DH], both[:, DH:]]
    return out


def odd_rows(value, size):
    return below(*[value[i : i + size] for i in range(size, value.shape[0], 2 * size)])


def less_odd_rows(value, change, size):
    parts = []
    for n, i in enumerate(range(0, value.shape[0], 2 * size)):
        parts += [value[i : i + size], value[i + size : i + 2 * size] - change[n * size : (n + 1) * size]]
    return below(*parts)


def split_three(g):
    high = g.astype(BF16)
    rest = g - high.astype(F32)
    mid = rest.astype(BF16)
    low = (rest - mid.astype(F32)).astype(BF16)
    return high, mid, low


def pack_gain(g):
    row = lax.broadcasted_iota(jnp.int32, (WIRE - DH, DH), 0)
    high, mid, low = split_three(g)
    block = jnp.where(
        row == 0,
        high.astype(F32),
        jnp.where(row == 1, mid.astype(F32), jnp.where(row == 2, low.astype(F32), 0.0)),
    )
    return block.astype(BF16)


def unpack_gain(block):
    rows = block.astype(F32)
    return rows[0:1] + rows[1:2] + rows[2:3]


def gate_rows(heads, ld, be):
    rows = below(ld, be)
    cum = rows
    for steps in (1, 2, 4, 8, 16, 32, 64):
        cum = cum + shift_lanes(cum, steps)
    row8 = lax.broadcasted_iota(jnp.int32, (2 * heads, CHUNK), 0)
    return jnp.where(row8 < heads, cum, rows)


def prep_kernel(
    heads, per, ld_ref, be_ref, k_ref, q_ref, m_ref, ke_ref, qe_ref, qf_ref, e_ref, g_ref, w_ref, f_scr, gp_scr
):
    step = pl.program_id(0)

    @pl.when(step == 0)
    def _():
        f_scr[...] = jnp.zeros_like(f_scr)
        gp_scr[...] = jnp.ones_like(gp_scr)

    ti = lax.broadcasted_iota(jnp.int32, (CHUNK, CHUNK), 0)
    tj = lax.broadcasted_iota(jnp.int32, (CHUNK, CHUNK), 1)
    eye = jnp.where(ti == tj, 1.0, 0.0)
    state = []
    ts = []
    products = []
    diags = []
    for c in range(per):
        part = slice(c * CHUNK, (c + 1) * CHUNK)
        rows = gate_rows(heads, ld_ref[:, part], be_ref[:, part])
        cols = jnp.transpose(rows)
        keys = []
        colmat = jnp.zeros((CHUNK, CHUNK), F32)
        for h in range(heads):
            k = k_ref[part, h * DH : (h + 1) * DH]
            kf = k.astype(F32)
            rk = lax.rsqrt(jnp.sum(kf * kf, axis=1, keepdims=True) + 1e-6)
            keys.append((k, kf, rk))
            colmat = jnp.where(tj == h, rk, colmat)
        rowmat = jnp.transpose(colmat)
        for h in range(0, heads, 2):
            two = slice(h * DH, (h + 2) * DH)
            kd = diagonal(keys[h][0], keys[h + 1][0])
            diags.append(kd)
            kk2 = dot(k_ref[part, two], kd, NT)
            qk2 = dot(q_ref[part, two], kd, NT)
            products.append((kk2[:, :CHUNK], qk2[:, :CHUNK]))
            products.append((kk2[:, CHUNK:], qk2[:, CHUNK:]))
        for h in range(heads):
            k, kf, rk_c = keys[h]
            kk, qk = products[c * heads + h]
            rk_r = rowmat[h : h + 1]
            qf = q_ref[part, h * DH : (h + 1) * DH].astype(F32)
            rq_c = lax.rsqrt(jnp.sum(qf * qf, axis=1, keepdims=True) + 1e-6)
            g_c = cols[:, h : h + 1]
            g_r = rows[h : h + 1]
            b_c = cols[:, heads + h : heads + h + 1]
            b_r = rows[heads + h : heads + h + 1]
            decay = jnp.exp(jnp.where(ti >= tj, g_c - g_r, NEG)) * rk_r
            a = beside(*halves(decay * rq_c * qk))
            low = jnp.where(ti > tj, decay * (b_c * rk_c) * kk, 0.0)
            ts.append(eye - jnp.where((ti >> 1) == (tj >> 1), low, 0.0))
            state.append((kf, rk_c, rk_r, qf, rq_c, g_c, g_r, b_r, a, low))
    count = per * heads
    for shift in range(1, 7):
        pair = (ti >> (shift + 1)) == (tj >> (shift + 1))
        cross = pair & (((ti >> shift) & 1) == 1) & (((tj >> shift) & 1) == 0)
        size = 1 << shift
        tb = [t.astype(BF16) for t in ts]
        lead = [odd_rows(t, size).astype(BF16) for t in ts] if size >= 8 else tb
        lm = [below(*halves(jnp.where(cross, s[-1], 0.0))) for s in state]
        mid = [dot(beside(x, x), y).astype(BF16) for x, y in zip(lead, lm)]
        change = []
        for n in range(0, count, 2):
            both = dot(beside(mid[n], mid[n + 1]), diagonal(tb[n], tb[n + 1]))
            change += [both[:, :CHUNK], both[:, CHUNK:]]
        if size >= 8:
            ts = [less_odd_rows(t, x, size) for t, x in zip(ts, change)]
        else:
            ts = [t - x for t, x in zip(ts, change)]
    ws = []
    for n in range(0, count, 2):
        lead = []
        for s, t in zip(state[n : n + 2], ts[n : n + 2]):
            lead.append((t * (s[7] * jnp.exp(s[6]) * s[2])).astype(BF16))
        both = dot(beside(*lead), diags[n // 2])
        ws += [both[:, :DH], both[:, DH:]]
    starts = []
    for n in range(count):
        c, h = n // heads, n % heads
        kf, rk_c, rk_r, qf, rq_c, g_c, g_r, b_r, a, low = state[n]
        t, w = ts[n], ws[n]
        tail_c = jnp.exp(g_r[:, CHUNK - 1 : CHUNK] - g_c) * rk_c
        tw = beside(t.astype(BF16), w.astype(BF16))
        both = dot(a, below(tw, tw))
        m_ref[c, h] = (both[:, :CHUNK] * b_r).astype(BF16)
        qe = (jnp.exp(g_c) * rq_c) * qf - both[:, CHUNK:]
        kt = jnp.transpose(kf).astype(BF16)
        th, tl = halves(tail_c * t * b_r)
        wh, wl = halves(tail_c * w)
        both = dot(beside(kt, kt), below(beside(th, wh), beside(tl, wl)))
        ke_ref[c, h] = beside(*halves(both[:, :CHUNK]))
        e = -both[:, CHUNK:]
        qeb, eb = qe.astype(BF16), e.astype(BF16)
        qe_ref[c, h] = qeb
        e_ref[c, h] = eb
        starts.append((qe, e, below(qeb, eb), jnp.broadcast_to(jnp.exp(g_r[:, CHUNK - 1 : CHUNK]), (1, DH))))
    for c in range(per):
        for h in range(0, heads, 2):
            ones = starts[c * heads + h : c * heads + h + 2]
            fs = [f_scr[h], f_scr[h + 1]]
            both = dot(beside(ones[0][2], ones[1][2]), diagonal(fs[0].astype(BF16), fs[1].astype(BF16)))
            for n, (qe, e, _, gc) in enumerate(ones):
                part = both[:, n * DH : (n + 1) * DH]
                gp = gp_scr[h + n : h + n + 1]
                qf_ref[c, h + n] = beside(*halves(gp * qe + part[:CHUNK]))
                f_scr[h + n] = gc * fs[n] + gp * e + part[CHUNK:]
                gp_scr[h + n : h + n + 1] = gp * gc
                g_ref[c, h + n : h + n + 1] = gc

    @pl.when(step == pl.num_programs(0) - 1)
    def _():
        for h in range(heads):
            matrix = jnp.transpose(f_scr[h]).astype(BF16)
            gain = pack_gain(gp_scr[h : h + 1])
            for copy in range(w_ref.shape[0] // heads):
                w_ref[h * (w_ref.shape[0] // heads) + copy, :DH] = matrix
                w_ref[h * (w_ref.shape[0] // heads) + copy, DH:] = gain


PER = 4


def prep(log_decay, beta, delta_key, delta_query, copies):
    heads, rows = log_decay.shape
    chunks = rows // CHUNK
    big = jax.ShapeDtypeStruct((chunks, heads, CHUNK, DH), BF16)
    wide = jax.ShapeDtypeStruct((chunks, heads, CHUNK, 2 * DH), BF16)
    big_spec = pl.BlockSpec((PER, heads, CHUNK, DH), lambda c: (c, 0, 0, 0))
    wide_spec = pl.BlockSpec((PER, heads, CHUNK, 2 * DH), lambda c: (c, 0, 0, 0))
    row_spec = pl.BlockSpec((heads, PER * CHUNK), lambda c: (0, c))
    tok_spec = pl.BlockSpec((PER * CHUNK, heads * DH), lambda c: (c, 0))
    return pl.pallas_call(
        functools.partial(prep_kernel, heads, PER),
        grid=(chunks // PER,),
        in_specs=[row_spec, row_spec, tok_spec, tok_spec],
        out_specs=[big_spec, wide_spec, big_spec, wide_spec, big_spec]
        + [
            pl.BlockSpec((PER, heads, DH), lambda c: (c, 0, 0)),
            pl.BlockSpec((heads * copies, WIRE, DH), lambda c: (0, 0, 0)),
        ],
        out_shape=[big, wide, big, wide, big]
        + [
            jax.ShapeDtypeStruct((chunks, heads, DH), F32),
            jax.ShapeDtypeStruct((heads * copies, WIRE, DH), BF16),
        ],
        scratch_shapes=[pltpu.VMEM((heads, DH, DH), F32), pltpu.VMEM((heads, DH), F32)],
        compiler_params=pltpu.CompilerParams(vmem_limit_bytes=VMEM),
        cost_estimate=pl.CostEstimate(flops=1_000_000, bytes_accessed=1_000_000, transcendentals=0),
        name="delta_prep",
    )(log_decay, beta, delta_key, delta_query)


QB = 256
SCALE = 1.0 / math.sqrt(DH) * math.log2(math.e)


def own_kernel(q_ref, k_ref, v_ref, o_ref, vx):
    rows = q_ref.shape[0]
    vx[:, :DH] = v_ref[...]
    vx[:, DH:] = jnp.ones((rows, DH), BF16)
    ri = lax.broadcasted_iota(jnp.int32, (QB, QB), 0)
    rj = lax.broadcasted_iota(jnp.int32, (QB, QB), 1)
    lane = lax.broadcasted_iota(jnp.int32, (QB, DH), 1)
    blocks = [slice(i * QB, (i + 1) * QB) for i in range(rows // QB)]
    scores = []
    for here in blocks:
        s = dot(q_ref[here], k_ref[: here.stop], NT)
        edge = jnp.where(rj <= ri, s[:, here], NEG)
        scores.append(beside(s[:, : here.start], edge) if here.start else edge)
    for here, s in zip(blocks, scores):
        top = jnp.max(s, axis=1, keepdims=True)
        pv = dot(jnp.exp2((s - top) * SCALE).astype(BF16), vx[: here.stop])
        o_ref[here, :DH] = pv[:, :DH]
        o_ref[here, DH:] = jnp.where(lane < DH // 2, pv[:, DH:], top)


def own_part(att_query, att_key, att_value):
    rows, width = att_query.shape
    heads = width // DH
    tok = pl.BlockSpec((rows, DH), lambda h: (0, h))
    return pl.pallas_call(
        own_kernel,
        grid=(heads,),
        in_specs=[tok, tok, tok],
        out_specs=pl.BlockSpec((rows, 2 * DH), lambda h: (0, h)),
        out_shape=jax.ShapeDtypeStruct((rows, 2 * width), F32),
        scratch_shapes=[pltpu.VMEM((rows, 2 * DH), BF16)],
        compiler_params=pltpu.CompilerParams(vmem_limit_bytes=VMEM),
        cost_estimate=pl.CostEstimate(flops=100_000_000_000, bytes_accessed=1_000_000, transcendentals=0),
        name="own_attention",
    )(att_query, att_key, att_value)


def attend_kernel(
    base, first_ref, q_ref, kp_ref, ko_ref, vp_ref, own_ref, m_ref, ke_ref, qe_ref, e_ref, g_ref, *rest
):
    r_ref, b_ref, kx, vx = rest[-4:]
    h = pl.program_id(0) + base
    first = first_ref[0]
    window = kp_ref.shape[0]
    vx[:, :DH] = vp_ref[...]

    @pl.when(first == 0)
    def _():
        kx[...] = kp_ref[...]
        vx[:, DH:] = jnp.ones((window, DH), BF16)

    @pl.when(first != 0)
    def _():
        kx[...] = jnp.broadcast_to(ko_ref[0:1].astype(F32), (window, DH)).astype(BF16)
        vx[:, DH:] = jnp.zeros((window, DH), BF16)

    ri = lax.broadcasted_iota(jnp.int32, (QB, QB), 0)
    rj = lax.broadcasted_iota(jnp.int32, (QB, QB), 1)
    blocks = [slice(i * QB, (i + 1) * QB) for i in range(q_ref.shape[0] // QB)]
    scores = []
    for i, here in enumerate(blocks):
        s = dot(q_ref[here], kx[i * QB :], NT)
        edge = jnp.where(rj > ri, s[:, :QB], NEG)
        scores.append(beside(edge, s[:, QB:]) if s.shape[1] > QB else edge)
    sums = []
    for i, (here, s) in enumerate(zip(blocks, scores)):
        own_top = own_ref[here, 2 * DH - 1 :]
        top = jnp.maximum(jnp.max(s, axis=1, keepdims=True), own_top)
        pv = dot(jnp.exp2((s - top) * SCALE).astype(BF16), vx[i * QB :])
        sums.append((pv, jnp.exp2((own_top - top) * SCALE)))
    outs = []
    for here, (pv, fade) in zip(blocks, sums):
        total = pv[:, DH:] + fade * own_ref[here, DH : DH + 1]
        outs.append(((pv[:, :DH] + fade * own_ref[here, :DH]) / total).astype(BF16).astype(F32))
    squares = mean_squares(outs)
    values = [halves(o * lax.rsqrt(square + 1e-6)) for o, square in zip(outs, squares)]
    per = QB // CHUNK
    chunks = []
    for c in range(m_ref.shape[0]):
        part = slice((c % per) * CHUNK, (c % per + 1) * CHUNK)
        chunks.append((values[c // per][0][part], values[c // per][1][part]))
    fresh = []
    for c, (vh, vl) in enumerate(chunks):
        ke = ke_ref[c, 0]
        fresh.append(dot(ke, below(vh, vh)) + dot(ke[:, :DH], vl))
    x = jnp.zeros((DH, DH), F32)
    states = []
    for c in range(len(chunks)):
        xh, xl = halves(x)
        states.append(below(xh, xl))
        x = g_ref[c, pl.ds(h, 1)] * x + dot(e_ref[c, 0], xh) + fresh[c]
    for c, (vh, vl) in enumerate(chunks):
        m, qe = m_ref[c, 0], qe_ref[c, 0]
        r_ref[c * CHUNK : (c + 1) * CHUNK] = dot(beside(m, m), below(vh, vl)) + dot(beside(qe, qe), states[c])
    b_ref[0] = jnp.transpose(x).astype(BF16)


def attend(base, first, att_query, kv_prev, k_own, own, m, ke, qe, e, g, *earlier):
    rows, width = att_query.shape
    heads = width // DH
    window, held = kv_prev.shape
    held = held // (2 * DH)
    chunks = rows // CHUNK
    big = pl.BlockSpec((chunks, 1, CHUNK, DH), lambda h: (0, h + base, 0, 0))
    tok = pl.BlockSpec((rows, DH), lambda h: (0, h + base))
    return pl.pallas_call(
        functools.partial(attend_kernel, base),
        grid=(held,),
        in_specs=[
            pl.BlockSpec(memory_space=pltpu.SMEM),
            tok,
            pl.BlockSpec((window, DH), lambda h: (0, h)),
            pl.BlockSpec((16, DH), lambda h: (0, h + base)),
            pl.BlockSpec((window, DH), lambda h: (0, h + held)),
            pl.BlockSpec((rows, 2 * DH), lambda h: (0, h + base)),
            big,
            pl.BlockSpec((chunks, 1, CHUNK, 2 * DH), lambda h: (0, h + base, 0, 0)),
            big,
            big,
            pl.BlockSpec((chunks, heads, DH), lambda h: (0, 0, 0)),
        ]
        + [pl.BlockSpec(memory_space=pl.ANY)] * len(earlier),
        out_specs=[tok, pl.BlockSpec((1, DH, DH), lambda h: (h + base, 0, 0))],
        out_shape=[
            jax.ShapeDtypeStruct((rows, width), F32),
            jax.ShapeDtypeStruct((heads, DH, DH), BF16),
        ],
        input_output_aliases={11 + n: n for n in range(len(earlier))},
        scratch_shapes=[pltpu.VMEM((window, DH), BF16), pltpu.VMEM((window, 2 * DH), BF16)],
        compiler_params=pltpu.CompilerParams(vmem_limit_bytes=LATER if earlier else MIDDLE),
        cost_estimate=pl.CostEstimate(flops=1_000_000 if earlier else 100_000_000_000, bytes_accessed=1_000_000, transcendentals=0),
        name="window_attention",
    )(first, att_query, kv_prev, k_own, kv_prev, own, m, ke, qe, e, g, *earlier)


def vmem_call(kernel, outs, name, *args):
    vm = pl.BlockSpec(memory_space=pltpu.VMEM)
    return pl.pallas_call(
        kernel,
        in_specs=[vm] * len(args),
        out_specs=[vm] * len(outs),
        out_shape=[jax.ShapeDtypeStruct(*o) for o in outs],
        compiler_params=pltpu.CompilerParams(vmem_limit_bytes=SMALL),
        cost_estimate=pl.CostEstimate(flops=1_000_000, bytes_accessed=1_000_000, transcendentals=0),
        name=name,
    )(*args)


def follow(g, f, d_ref):
    d = d_ref[:DH]
    step = unpack_gain(d_ref[DH:])
    return g * step, step * f + g * d.astype(F32) + dot(f.astype(BF16), d)


def prefix_kernel(d_ref, p_ref, t_ref):
    g = jnp.ones((1, DH), F32)
    f = jnp.zeros((DH, DH), F32)
    count = d_ref.shape[0]
    for z in range(count):
        p_ref[z, :DH] = f.astype(BF16)
        p_ref[z, DH:] = pack_gain(g)
        g, f = follow(g, f, d_ref.at[z])
    t_ref[:DH] = f.astype(BF16)
    t_ref[DH:] = pack_gain(g)


def line_kernel(d_ref, t_ref, b_ref, q_ref, w_ref):
    acc = b_ref[0].astype(F32)
    q_ref[0] = jnp.zeros_like(acc)
    for z in range(1, d_ref.shape[0]):
        q_ref[z] = acc
        g = unpack_gain(d_ref[z, DH:])
        acc = g * acc + b_ref[z].astype(F32) + dot(acc.astype(BF16), d_ref[z, :DH])
    size = acc.shape[0]
    wire = below(*halves(acc), t_ref[...])
    for x in range(w_ref.shape[0]):
        w_ref[x] = wire


def place_kernel(w_ref, earlier_ref, p_ref, q_ref, s_ref):
    size = q_ref.shape[1]
    base = jnp.zeros((size, DH), F32)
    for x in range(w_ref.shape[0] - 1):
        added = w_ref[x, :size].astype(F32) + w_ref[x, size : 2 * size].astype(F32)
        if x:
            step = unpack_gain(w_ref[x, 2 * size + DH :])
            added = added + step * base + dot(base.astype(BF16), w_ref[x, 2 * size : 2 * size + DH])
        base = jnp.where(earlier_ref[x : x + 1] > 0.0, added, base)
    high = base.astype(BF16)
    for z in range(p_ref.shape[0]):
        out = unpack_gain(p_ref[z, DH:]) * base + q_ref[z] + dot(high, p_ref[z, :DH])
        s_ref[z] = out.astype(BF16)


def finish_kernel(heads, r_ref, qf_ref, s_ref, gate_ref, gain_ref, o_ref):
    gain = gain_ref[...]
    tiles = [
        (slice(c * CHUNK, (c + 1) * CHUNK), slice(h * DH, (h + 1) * DH), c, h)
        for c in range(qf_ref.shape[0])
        for h in range(heads)
    ]
    reads = [r_ref[rows, cols] + dot(qf_ref[c, h], beside(s_ref[h], s_ref[h]), NT) for rows, cols, c, h in tiles]
    squares = mean_squares(reads)
    for (rows, cols, c, h), r, square in zip(tiles, reads, squares):
        gate = gate_ref[rows, cols].astype(F32)
        r = r * lax.rsqrt(square + 1e-6) * gain
        o_ref[rows, cols] = (r * (gate / (1.0 + jnp.exp(-gate)))).astype(BF16)


def finish(readout, qf, state, out_gate, gain):
    rows, width = readout.shape
    heads = width // DH
    tok = pl.BlockSpec((PER * CHUNK, width), lambda c: (c, 0))
    return pl.pallas_call(
        functools.partial(finish_kernel, heads),
        grid=(rows // (PER * CHUNK),),
        in_specs=[
            tok,
            pl.BlockSpec((PER, heads, CHUNK, 2 * DH), lambda c: (c, 0, 0, 0)),
            pl.BlockSpec((heads, DH, DH), lambda c: (0, 0, 0)),
            tok,
            pl.BlockSpec((1, DH), lambda c: (0, 0)),
        ],
        out_specs=tok,
        out_shape=jax.ShapeDtypeStruct((rows, width), BF16),
        compiler_params=pltpu.CompilerParams(vmem_limit_bytes=VMEM),
        cost_estimate=pl.CostEstimate(flops=140_000_000, bytes_accessed=6_000_000, transcendentals=600_000),
        name="gated_readout",
    )(readout, qf, state, out_gate, gain)


def body(att_query, att_key, att_value, delta_query, delta_key, out_gate, log_decay, beta, norm_gain):
    heads = log_decay.shape[0]
    count = lax.axis_size("seq")
    minor = 2 * heads
    majors = count // minor
    place = lax.axis_index("seq")
    onward = [(s, s + 1) for s in range(count - 1)]
    copies = minor // heads
    last = heads - 1


    def both(begin, end):
        part = slice(begin * DH, end * DH)
        return beside(att_key[:, part], att_value[:, part])

    kv_first = lax.ppermute(both(0, last), "seq", onward)
    own = own_part(att_query, att_key, att_value)
    earlier = (jnp.arange(majors) < place // minor).astype(F32)
    earlier = jnp.broadcast_to(earlier[:, None], (majors, DH))
    own, kv_last, delta_key, earlier = lax.optimization_barrier((own, both(last, heads), delta_key, earlier))
    kv_last = lax.ppermute(kv_last, "seq", onward)
    m, ke, qe, qf, e, g, wire = prep(log_decay, beta, delta_key, delta_query, copies)
    lines = [[x * minor + z for z in range(minor)] for x in range(majors)]
    d_line = lax.all_to_all(wire, "seq", 0, 0, axis_index_groups=lines)
    first = jnp.reshape((place == 0).astype(jnp.int32), (1,))
    coefs = (own, m, ke, qe, e, g)
    early = attend(0, first, att_query, kv_first, att_key, *coefs)
    readout, b = attend(last, first, att_query, kv_last, att_key, *coefs, *early)
    d_line, b = lax.optimization_barrier((d_line, b))
    p_line, d_total = vmem_call(
        prefix_kernel, [(d_line.shape, BF16), (d_line.shape[1:], BF16)], "decay_prefix", d_line
    )
    b, p_line, d_total = lax.optimization_barrier((b, p_line, d_total))
    size = DH // copies
    b_line = lax.all_to_all(b.reshape(minor, size, DH), "seq", 0, 0, axis_index_groups=lines)
    q_line, added = vmem_call(
        line_kernel, [(b_line.shape, F32), ((majors, 2 * size + WIRE, DH), BF16)], "line_states", d_line, d_total, b_line
    )

    columns = [[x * minor + z for x in range(majors)] for z in range(minor)]
    wires = lax.all_to_all(added, "seq", 0, 0, axis_index_groups=columns)
    (s_line,) = vmem_call(place_kernel, [(b_line.shape, BF16)], "block_states", wires, earlier, p_line, q_line)
    state = lax.all_to_all(s_line, "seq", 0, 0, axis_index_groups=lines).reshape(heads, DH, DH)
    return finish(readout, qf, state, out_gate, norm_gain.reshape(1, DH))


def solution(mesh):
    tokens = P(("doc", "seq"), "head")
    gates = P("head", ("doc", "seq"))
    return jax.shard_map(
        body,
        mesh=mesh,
        in_specs=(tokens,) * 6 + (gates, gates, P()),
        out_specs=tokens,
        check_vma=False,
    )
```
